32 devices in a mesh: row: 8 (over z, y), col: 4 (over x, core).
Axes of the slice: x: 2, y: 2, z: 4, core: 2. Of those that a mesh axis runs over, the one named last changes fastest.
Arguments:
- tokens: bfloat16 [1024, 4096], P('row', 'col'), may hold values from -6 to 6
- w_in: bfloat16 [4096, 16384], P('col', 'row'), may hold values from -0.09375 to 0.09375
- w_out: bfloat16 [16384, 4096], P('row', 'col'), may hold values from -0.046875 to 0.046875
- cotangent: bfloat16 [1024, 4096], P('row', 'col'), may hold values from -6 to 6
Outputs:
- block_out: bfloat16 [1024, 4096], P(('row', 'col'))
- grad_tokens: bfloat16 [1024, 4096], P('row', 'col')
- grad_in: float32 [4096, 16384], P('col', 'row')
- grad_out: float32 [16384, 4096], P('row', 'col')
The draws below stay inside these ranges and needn't reach their ends.
All inputs are finite; a program needn't handle non-finite values.
Results may differ from the reference program's by a relative error of at most 0.015.
Values may be sent and summed in bfloat16 or wider, within the bound.
No kernel may reach another device: no remote copies, remote signals or barrier semaphores. Data moves between devices by JAX's collectives and lax.ppermute only.
A program may use at most 128 MiB of HBM per device.

```python
import jax
import jax.numpy as jnp
from jax import lax

D = 4096
F = 16384
TOKENS = 1024
N_ROW = 8
N_COL = 4


def level_of(key, extent, cuts, least, high):
    level, own = 1.0, jax.random.fold_in(key, 6)
    for position, blocks in cuts:
        steps = jnp.exp(jax.random.uniform(jax.random.fold_in(own, position), (blocks,), jnp.float32, least / len(cuts), high / len(cuts)))
        level = level * jnp.repeat(steps, extent[position] // blocks).reshape([-1 if axis == position else 1 for axis in range(len(extent))])
    return level


def centred(stream_key, extent, scale, limit, pieces=(), dtype=jnp.bfloat16):
    gain = level_of(stream_key, extent, pieces, -0.22, 0.18) if pieces else 1.0
    result = jax.random.normal(stream_key, extent, jnp.float32) * scale * gain
    return jnp.minimum(jnp.maximum(result, -limit), limit).astype(dtype)


def setup_inputs(seed: int = 0) -> dict:
    keys = jax.random.split(jax.random.key(seed), 5)
    return {
        "tokens": centred(keys[0], (TOKENS, D), 1.0, 6.0, ((0, 8), (1, 4))),
        "w_in": centred(keys[1], (D, F), D ** -0.5, 0.09375, ((0, 4), (1, 8))),
        "w_out": centred(keys[2], (F, D), F ** -0.5, 0.046875, ((0, 8), (1, 4))),
        "cotangent": centred(keys[3], (TOKENS, D), 1.0, 6.0, ((0, 8), (1, 4))),
    }


def block_sum(left, right, parts):
    width = left.shape[1] // parts
    total = jnp.zeros((left.shape[0], right.shape[1]), jnp.float32)
    for index in range(parts):
        piece = jnp.dot(left[:, index * width:(index + 1) * width], right[index * width:(index + 1) * width], preferred_element_type=jnp.float32)
        rounded = lax.optimization_barrier(piece.astype(jnp.bfloat16))
        total = total + rounded.astype(jnp.float32)
    return total

def gelu_grad(value):
    cdf = 0.5 * (1.0 + jax.scipy.special.erf(value * 0.7071067811865476))
    pdf = jnp.exp(-0.5 * value * value) * 0.3989422804014327
    return cdf + value * pdf

def reference(tokens, w_in, w_out, cotangent):
    pre = block_sum(tokens, w_in, N_COL)
    act = jax.nn.gelu(pre, approximate=False).astype(jnp.bfloat16)
    block_out = (tokens.astype(jnp.float32) + block_sum(act, w_out, N_ROW)).astype(jnp.bfloat16)
    dact = block_sum(cotangent, w_out.T, N_COL)
    dpre = (dact * gelu_grad(pre)).astype(jnp.bfloat16)
    grad_out = jnp.dot(act.T, cotangent, preferred_element_type=jnp.float32)
    grad_in = jnp.dot(tokens.T, dpre, preferred_element_type=jnp.float32)
    grad_tokens = (cotangent.astype(jnp.float32) + block_sum(dpre, w_in.T, N_ROW)).astype(jnp.bfloat16)
    return (block_out, grad_tokens, grad_in, grad_out)
```

```python
import jax
import jax.numpy as jnp
from jax import lax
from jax.sharding import PartitionSpec as P

CORES = 2
F32 = jnp.float32
BF16 = jnp.bfloat16


def ring_order(count):
    if count % 4:
        return list(range(count))
    minor = count // 4
    order = [major * minor for major in range(4)]
    for turn, major in enumerate(reversed(range(4))):
        steps = range(1, minor) if turn % 2 == 0 else range(minor - 1, 0, -1)
        order += [major * minor + step for step in steps]
    return order


def ring_pairs(count, n_col, sign):
    order = ring_order(count)
    pairs = []
    for place in range(count):
        for col in range(n_col):
            step = sign if col % CORES == 0 else -sign
            target = order[(place + step) % count]
            pairs.append((order[place] * n_col + col, target * n_col + col))
    return pairs


def gelu_parts(value):
    cdf = 0.5 * (1.0 + lax.erf(value * 0.7071067811865476))
    pdf = jnp.exp(-0.5 * value * value) * 0.3989422804014327
    return (value * cdf).astype(BF16), (cdf + value * pdf).astype(BF16)


def dot_nn(left, right):
    return jnp.dot(left, right, preferred_element_type=F32)


def dot_nt(left, right):
    return lax.dot_general(left, right, (((1,), (1,)), ((), ())), preferred_element_type=F32)


def dot_tn(left, right):
    return lax.dot_general(left, right, (((0,), (0,)), ((), ())), preferred_element_type=F32)


def solution(mesh):
    n_row, n_col = mesh.shape["row"], mesh.shape["col"]
    n_x = n_col // CORES
    far = n_row // 2
    ring_a = ring_pairs(n_row, n_col, 1)
    ring_b = ring_pairs(n_row, n_col, -1)
    sibling = [(col, col ^ 1) for col in range(n_col)]
    chip_ring = [(col, (col + CORES) % n_col) for col in range(n_col)]

    def along(value, pairs):
        return lax.ppermute(value, ("row", "col"), pairs)

    def to_sibling(value):
        return lax.ppermute(value, "col", sibling)

    def local(tokens, w_in, w_out, cotangent):
        half = tokens.shape[0] // 2
        core = lax.axis_index("col") % CORES

        def shares(block):
            low, high = block[:half], block[half:]
            return jnp.where(core == 0, low, high), jnp.where(core == 0, high, low)

        def joined(mine, other):
            return jnp.concatenate([jnp.where(core == 0, mine, other), jnp.where(core == 0, other, mine)])

        def gather(block):
            mine, other = shares(block)
            a, b = [mine], [other]
            cur_a = cur_b = block
            for step in range(1, far + 1):
                if step == far:
                    cur_a, cur_b = shares(cur_a)[0], shares(cur_b)[1]
                cur_a, cur_b = along(cur_a, ring_a), along(cur_b, ring_b)
                a.append(cur_a)
                b.append(cur_b)
            return a, b

        def width_sum(mine, other, product):
            got = to_sibling(product(other).astype(BF16))
            chip = (product(mine) + got.astype(F32)).astype(BF16)
            total = chip.astype(F32)
            for _ in range(n_x - 1):
                chip = lax.ppermute(chip, "col", chip_ring)
                total = total + chip.astype(F32)
            return total

        def unit_sum(share_a, share_b, product, own):
            go_a = along(product(share_b[far]).astype(BF16), ring_a)
            go_b = along(product(share_a[far]).astype(BF16), ring_b)
            for step in range(far - 1, 0, -1):
                part_a, part_b = product(share_b[step]), product(share_a[step])
                if step == far - 1:
                    pad = jnp.zeros_like(go_a)
                    go_a, go_b = joined(pad, go_a), joined(go_b, pad)
                go_a = along((part_a + go_a.astype(F32)).astype(BF16), ring_a)
                go_b = along((part_b + go_b.astype(F32)).astype(BF16), ring_b)
            rest = product(joined(share_a[0], share_b[0]))
            total = own.astype(F32) + rest + go_a.astype(F32) + go_b.astype(F32)
            return total.astype(BF16)

        tok_a, tok_b = gather(tokens)
        cot_a, cot_b = gather(cotangent)

        act_a, act_b, slope_a = {}, {}, {}
        for step in range(far + 1):
            pre = width_sum(tok_a[step], tok_b[step], lambda rows: dot_nn(rows, w_in))
            act_a[step], slope_a[step] = gelu_parts(pre)
            act_b[step] = to_sibling(act_a[step])

        mixed = unit_sum(act_a, act_b, lambda rows: dot_nn(rows, w_out), tokens)
        block_out = lax.all_to_all(mixed, "col", split_axis=0, concat_axis=1, tiled=True)

        dpre_a, dpre_b = {}, {}
        for step in range(far, -1, -1):
            dact = width_sum(cot_a[step], cot_b[step], lambda rows: dot_nt(rows, w_out))
            dpre_a[step] = (dact * slope_a[step].astype(F32)).astype(BF16)
            dpre_b[step] = to_sibling(dpre_a[step])

        back = unit_sum(dpre_a, dpre_b, lambda rows: dot_nt(rows, w_in), cotangent)

        def whole(a, b):
            return jnp.concatenate([p for step in range(far + 1) for p in (a[step], b[step])])

        grad_out = dot_tn(whole(act_a, act_b), whole(cot_a, cot_b))
        grad_in = dot_tn(whole(tok_a, tok_b), whole(dpre_a, dpre_b))
        return block_out, back, grad_in, grad_out

    in_specs = (P("row", "col"), P("col", "row"), P("row", "col"), P("row", "col"))
    out_specs = (P(("row", "col"), None), P("row", "col"), P("col", "row"), P("row", "col"))
    return jax.shard_map(local, mesh=mesh, in_specs=in_specs, out_specs=out_specs, check_vma=False)
```

```python
import jax
import jax.numpy as jnp
from jax import lax
from jax.experimental import pallas as pl
from jax.experimental.pallas import tpu as pltpu
from jax.sharding import PartitionSpec as P

CORES = 2
F32 = jnp.float32
BF16 = jnp.bfloat16
MIB = 2 ** 20
IN_VMEM = pl.BlockSpec(memory_space=pltpu.VMEM)
ANYWHERE = pl.BlockSpec(memory_space=pl.ANY)
NOTHING = pl.CostEstimate(flops=0, bytes_accessed=0, transcendentals=0)


def ring_order(count):
    if count % 4:
        return list(range(count))
    minor = count // 4
    order = [major * minor for major in range(4)]
    for turn, major in enumerate(reversed(range(4))):
        steps = range(1, minor) if turn % 2 == 0 else range(minor - 1, 0, -1)
        order += [major * minor + step for step in steps]
    return order


def ring_pairs(count, n_col, sign):
    order = ring_order(count)
    pairs = []
    for place in range(count):
        for col in range(n_col):
            step = sign if col % CORES == 0 else -sign
            target = order[(place + step) % count]
            pairs.append((order[place] * n_col + col, target * n_col + col))
    return pairs


def shape(rows, columns):
    return jax.ShapeDtypeStruct((rows, columns), BF16)


def half_at(which, half):
    core = lax.axis_index("col") % CORES
    return pl.ds(pl.multiple_of((core if which == 0 else 1 - core) * half, half), half)


def multiply(rows, weight_ref, out_ref, out_rows=slice(None), add=None, tile=512):
    for start in range(0, weight_ref.shape[1], tile):
        piece = pl.ds(start, min(tile, weight_ref.shape[1] - start))
        part = jnp.dot(rows, weight_ref[:, piece], preferred_element_type=F32)
        if add is not None:
            part = part + add[:, piece].astype(F32)
        out_ref[out_rows, piece] = part.astype(BF16)


def strips(rows):
    return [pl.ds(start, 16) for start in range(0, rows, 16)]


class Chain:
    def __init__(self, first):
        self.last = first

    def run(self, name, body, outs, ins):
        def kernel(after_ref, *refs):
            body(refs[: len(ins)], refs[len(ins):])

        result = pl.pallas_call(
            kernel,
            out_shape=outs,
            in_specs=[ANYWHERE] + [IN_VMEM] * len(ins),
            out_specs=[IN_VMEM] * len(outs),
            compiler_params=pltpu.CompilerParams(vmem_limit_bytes=16 * MIB),
            cost_estimate=NOTHING,
            name=name,
        )(self.last, *ins)
        self.last = result[0]
        return result

    def outer(self, name, left, right):
        tile = min(512, left.shape[1])

        def kernel(after_ref, left_ref, right_ref, out_ref):
            band = pl.ds(pl.multiple_of(pl.program_id(0) * tile, tile), tile)
            out_ref[...] = lax.dot_general(
                left_ref[:, band], right_ref[...], (((0,), (0,)), ((), ())), preferred_element_type=F32
            )

        return pl.pallas_call(
            kernel,
            grid=(left.shape[1] // tile,),
            out_shape=jax.ShapeDtypeStruct((left.shape[1], right.shape[1]), F32),
            in_specs=[ANYWHERE, IN_VMEM, IN_VMEM],
            out_specs=pl.BlockSpec((tile, right.shape[1]), lambda band: (band, 0)),
            compiler_params=pltpu.CompilerParams(vmem_limit_bytes=24 * MIB),
            cost_estimate=NOTHING,
            name=name,
        )(self.last, left, right)


def solution(mesh):
    n_row, n_col = mesh.shape["row"], mesh.shape["col"]
    n_x = n_col // CORES
    far = n_row // 2
    ring_a = ring_pairs(n_row, n_col, 1)
    ring_b = ring_pairs(n_row, n_col, -1)
    sibling = [(col, col ^ 1) for col in range(n_col)]
    chip_ring = [(col, (col + CORES) % n_col) for col in range(n_col)]

    def along_a(value):
        return lax.ppermute(value, ("row", "col"), ring_a)

    def along_b(value):
        return lax.ppermute(value, ("row", "col"), ring_b)

    def to_sibling(value):
        return lax.ppermute(value, "col", sibling)

    def over_chips(value):
        parts = [value]
        for _ in range(n_x - 1):
            parts.append(lax.ppermute(parts[-1], "col", chip_ring))
        return parts

    def local(tokens, w_in, w_out, cotangent):
        rows, width = tokens.shape
        half = rows // 2
        units = w_in.shape[1]
        chain = Chain(tokens)

        own = jnp.concatenate([tokens, cotangent])
        a, b = {0: own}, {0: own}
        a[1], b[1] = along_a(own), along_b(own)

        def height(step):
            return rows if 0 < step < far else half

        def panel(ref, step, which, side):
            if step == 0:
                start = half_at(which, half)
                return ref[pl.ds(start.start + side * rows, half), :]
            return ref[side * height(step):(side + 1) * height(step), :]

        def relay(step):
            last = step + 1 == far

            def body(ins, outs):
                for which in range(2):
                    if last:
                        start = half_at(which, half)
                        for side in range(2):
                            outs[which][side * half:(side + 1) * half, :] = ins[which][
                                pl.ds(start.start + side * rows, half), :]
                    else:
                        outs[which][...] = ins[which][...]

            size = shape(rows if last else 2 * rows, width)
            go_a, go_b = chain.run("relay", body, [size, size], [a[step], b[step]])
            a[step + 1], b[step + 1] = along_a(go_a), along_b(go_b)

        got = {}

        def other(step, side, weight):
            def body(ins, outs):
                multiply(panel(ins[0], step, 1, side), ins[1], outs[0])

            product, = chain.run("other", body, [shape(height(step), units)], [b[step], weight])
            got[side, step] = to_sibling(product)

        sums = {}

        def mine(step, side, weight):
            def body(ins, outs):
                multiply(panel(ins[0], step, 0, side), ins[1], outs[0], add=ins[2])

            total, = chain.run("mine", body, [shape(height(step), units)], [a[step], weight, got[side, step]])
            sums[side, step] = over_chips(total)

        act_a, act_b, slope, dpre_a, dpre_b = {}, {}, {}, {}, {}

        def added(refs, strip):
            total = refs[0][strip, :].astype(F32)
            for ref in refs[1:]:
                total = total + ref[strip, :].astype(F32)
            return total

        def gelu(step):
            def body(ins, outs):
                for strip in strips(height(step)):
                    value = added(ins, strip)
                    cdf = 0.5 * (1.0 + lax.erf(value * 0.7071067811865476))
                    pdf = jnp.exp(-0.5 * value * value) * 0.3989422804014327
                    outs[0][strip, :] = (value * cdf).astype(BF16)
                    outs[1][strip, :] = (cdf + value * pdf).astype(BF16)

            size = shape(height(step), units)
            act_a[step], slope[step] = chain.run("gelu", body, [size, size], sums[0, step])
            act_b[step] = to_sibling(act_a[step])

        def slopes(step):
            def body(ins, outs):
                for strip in strips(height(step)):
                    value = added(ins[1:], strip) * ins[0][strip, :].astype(F32)
                    outs[0][strip, :] = value.astype(BF16)

            dpre_a[step], = chain.run("slopes", body, [shape(height(step), units)], [slope[step]] + sums[1, step])
            dpre_b[step] = to_sibling(dpre_a[step])

        terms = {}

        def term(step, side, share_a, share_b, weight):
            def body(ins, outs):
                if step == 0:
                    multiply(ins[0][...], ins[2], outs[0], half_at(0, half))
                    multiply(ins[1][...], ins[2], outs[0], half_at(1, half))
                else:
                    multiply(ins[1][...], ins[2], outs[0])
                    multiply(ins[0][...], ins[2], outs[1])

            outs = [shape(rows, width)] if step == 0 else [shape(height(step), width)] * 2
            terms[side, step] = chain.run("term", body, outs, [share_a[step], share_b[step], weight])

        moving = {}

        def reduce_hop(hop):
            parts = [(side, far - hop + side) for side in range(2) if 0 < far - hop + side <= far]
            before = [(side, far - hop + 1 + side) for side in range(2) if far - hop + 1 + side <= far]
            offsets, size = [], 0
            for _, step in parts:
                offsets.append(size)
                size += height(step)
            starts, total = {}, 0
            for side, step in before:
                starts[side] = total
                total += height(step)

            def body(ins, outs):
                for which in range(2):
                    for index, (side, step) in enumerate(parts):
                        base = offsets[index]
                        part = ins[2 * index + which]
                        if step == far:
                            outs[which][base:base + half, :] = part[...]
                            continue
                        came = ins[2 * len(parts) + which]
                        if step + 1 < far:
                            value = part[...].astype(F32) + came[starts[side]:starts[side] + rows, :].astype(F32)
                            outs[which][base:base + rows, :] = value.astype(BF16)
                            continue
                        touched, rest = half_at(1 - which, half), half_at(which, half)
                        value = part[touched, :].astype(F32) + came[starts[side]:starts[side] + half, :].astype(F32)
                        outs[which][pl.ds(touched.start + base, half), :] = value.astype(BF16)
                        outs[which][pl.ds(rest.start + base, half), :] = part[rest, :]

            ins = [value for part in parts for value in terms[part]]
            if hop:
                ins += moving[hop - 1]
            go_a, go_b = chain.run("hop", body, [shape(size, width)] * 2, ins)
            moving[hop] = [along_a(go_a), along_b(go_b)]

        def finish(side, residual, hop):
            def body(ins, outs):
                value = ins[0][...].astype(F32) + ins[1][...].astype(F32)
                value = value + ins[2][0:rows, :].astype(F32) + ins[3][0:rows, :].astype(F32)
                outs[0][...] = value.astype(BF16)

            result, = chain.run("finish", body, [shape(rows, width)], [residual, terms[side, 0][0]] + moving[hop])
            return result

        def turned(weight):
            def body(ins, outs):
                for start in range(0, weight.shape[0], 256):
                    outs[0][:, start:start + 256] = ins[0][start:start + 256, :].T

            return chain.run("turned", body, [shape(weight.shape[1], weight.shape[0])], [weight])[0]

        def whole(first, second):
            return jnp.concatenate([p for step in range(far + 1) for p in (first(step), second(step))])

        def side_of(blocks, step, which, side):
            if step:
                return blocks[step][side * height(step):(side + 1) * height(step)]
            core = lax.axis_index("col") % CORES
            block = own[side * rows:(side + 1) * rows]
            return jnp.where(core == which, block[:half], block[half:])

        def gathered(side):
            return whole(lambda step: side_of(a, step, 0, side), lambda step: side_of(b, step, 1, side))

        other(0, 0, w_in)
        w_out_t = turned(w_out)
        mine(0, 0, w_in)
        other(0, 1, w_out_t)
        w_in_t = turned(w_in)
        mine(0, 1, w_out_t)
        for step in range(1, far + 1):
            if step < far:
                relay(step)
            other(step, 0, w_in)
            if step == 1:
                gelu(0)
            else:
                term(step - 2, 0, act_a, act_b, w_out)
            mine(step, 0, w_in)
            if step == 1:
                slopes(0)
            elif step < far:
                gelu(step - 1)
        other(far, 1, w_out_t)
        term(0, 1, dpre_a, dpre_b, w_in_t)
        mine(far, 1, w_out_t)
        gelu(far - 1)
        for step in range(far - 1, 0, -1):
            other(step, 1, w_out_t)
            if step == far - 1:
                gelu(far)
                term(far - 1, 0, act_a, act_b, w_out)
            mine(step, 1, w_out_t)
            if step == far - 1:
                term(far, 0, act_a, act_b, w_out)
            reduce_hop(far - 1 - step)
            if step == far - 2 or far == 2:
                grad_out = chain.outer(
                    "grad_out", whole(act_a.__getitem__, act_b.__getitem__), gathered(1))
            slopes(step + 1)
            term(step + 1, 1, dpre_a, dpre_b, w_in_t)
        reduce_hop(far - 1)
        slopes(1)
        term(1, 1, dpre_a, dpre_b, w_in_t)
        reduce_hop(far)
        mixed = finish(0, tokens, far - 1)
        block_out = lax.all_to_all(mixed, "col", split_axis=0, concat_axis=1, tiled=True)
        grad_in = chain.outer("grad_in", gathered(0), whole(dpre_a.__getitem__, dpre_b.__getitem__))
        grad_tokens = finish(1, cotangent, far)
        return block_out, grad_tokens, grad_in, grad_out

    in_specs = (P("row", "col"), P("col", "row"), P("row", "col"), P("row", "col"))
    out_specs = (P(("row", "col"), None), P("row", "col"), P("col", "row"), P("row", "col"))
    return jax.shard_map(local, mesh=mesh, in_specs=in_specs, out_specs=out_specs, check_vma=False)
```

```python
import jax
import jax.numpy as jnp
from jax import lax
from jax.experimental import pallas as pl
from jax.experimental.pallas import tpu as pltpu
from jax.sharding import PartitionSpec as P

CORES = 2
F32 = jnp.float32
BF16 = jnp.bfloat16
MIB = 2 ** 20
IN_VMEM = pl.BlockSpec(memory_space=pltpu.VMEM)
ANYWHERE = pl.BlockSpec(memory_space=pl.ANY)
MICROSECOND = 10 ** 9
COSTS = {"grad_out": 6.0, "grad_in": 6.0, "grad_in_early": 6.0}
USUAL_COST = 3.0


def cost(name):
    return pl.CostEstimate(
        flops=int(COSTS.get(name, USUAL_COST) * MICROSECOND), bytes_accessed=0, transcendentals=0)


def ring_order(count):
    if count % 4:
        return list(range(count))
    minor = count // 4
    order = [major * minor for major in range(4)]
    for turn, major in enumerate(reversed(range(4))):
        steps = range(1, minor) if turn % 2 == 0 else range(minor - 1, 0, -1)
        order += [major * minor + step for step in steps]
    return order


def ring_pairs(count, n_col, sign):
    order = ring_order(count)
    pairs = []
    for place in range(count):
        for col in range(n_col):
            step = sign if col % CORES == 0 else -sign
            target = order[(place + step) % count]
            pairs.append((order[place] * n_col + col, target * n_col + col))
    return pairs


def shape(rows, columns):
    return jax.ShapeDtypeStruct((rows, columns), BF16)


def half_at(which, half, base=0):
    core = lax.axis_index("col") % CORES
    return pl.ds(pl.multiple_of((core if which == 0 else 1 - core) * half + base, half), half)


def tiles(extent, size):
    return [pl.ds(start, min(size, extent - start)) for start in range(0, extent, size)]


def added(refs, strip):
    total = refs[0][strip, :].astype(F32)
    for ref in refs[1:]:
        total = total + ref[strip, :].astype(F32)
    return total


def shifted(strip, offset):
    return pl.ds(strip.start + offset, strip.size)


class Chain:
    def __init__(self, first):
        self.last = first

    def run(self, name, body, outs, ins, holds=True):
        def kernel(after_ref, *refs):
            body(refs[: len(ins)], refs[len(ins):])

        result = pl.pallas_call(
            kernel,
            out_shape=outs,
            in_specs=[ANYWHERE] + [IN_VMEM] * len(ins),
            out_specs=[IN_VMEM] * len(outs),
            compiler_params=pltpu.CompilerParams(vmem_limit_bytes=8 * MIB),
            cost_estimate=cost(name),
            name=name,
        )(self.last, *ins)
        if holds:
            self.last = result[0]
        return result

    def outer(self, name, pairs, begun=None):
        tile = min(512, pairs[0][0].shape[1])
        arrays = [array for left, _, right, _ in pairs for array in (left, right)]
        out = jax.ShapeDtypeStruct((pairs[0][0].shape[1], pairs[0][2].shape[1]), F32)
        bands = pl.BlockSpec((tile, out.shape[1]), lambda band: (band, 0))
        more = [] if begun is None else [begun]

        def kernel(after_ref, *refs):
            band = pl.ds(pl.multiple_of(pl.program_id(0) * tile, tile), tile)
            total = None if begun is None else refs[len(arrays)][...]
            for index, (_, left_rows, _, right_rows) in enumerate(pairs):
                part = lax.dot_general(
                    refs[2 * index][left_rows, band], refs[2 * index + 1][right_rows, :],
                    (((0,), (0,)), ((), ())), preferred_element_type=F32)
                total = part if total is None else total + part
            refs[-2][...] = total
            refs[-1][...] = jnp.zeros_like(refs[-1])

        result, self.last = pl.pallas_call(
            kernel,
            grid=(out.shape[0] // tile,),
            out_shape=[out, shape(16, 128)],
            in_specs=[ANYWHERE] + [IN_VMEM] * len(arrays) + [bands] * len(more),
            out_specs=[bands, IN_VMEM],
            compiler_params=pltpu.CompilerParams(vmem_limit_bytes=24 * MIB),
            cost_estimate=cost(name),
            name=name,
        )(self.last, *arrays, *more)
        return result


def solution(mesh):
    n_row, n_col = mesh.shape["row"], mesh.shape["col"]
    n_x = n_col // CORES
    far = n_row // 2
    out_ring = ring_pairs(n_row, n_col, 1)
    back_ring = ring_pairs(n_row, n_col, -1)
    sibling = [(col, col ^ 1) for col in range(n_col)]
    chip_ring = [(col, (col + CORES) % n_col) for col in range(n_col)]

    def outward(value):
        return lax.ppermute(value, ("row", "col"), out_ring)

    def homeward(value):
        return lax.ppermute(value, ("row", "col"), back_ring)

    def to_sibling(value):
        return lax.ppermute(value, "col", sibling)

    def over_chips(value):
        parts = [value]
        for _ in range(n_x - 1):
            parts.append(lax.ppermute(parts[-1], "col", chip_ring))
        return parts

    def local(tokens, w_in, w_out, cotangent):
        rows, width = tokens.shape
        half = rows // 2
        units = w_in.shape[1]
        chain = Chain(tokens)
        order = [0] + list(range(far, 0, -1))

        def height(step):
            return rows if 0 < step < far else half

        share = sum(height(step) for step in order)

        def stacked():
            def body(ins, outs):
                outs[0][0:rows, :] = ins[0][...]
                outs[0][rows:2 * rows, :] = ins[1][...]

            return chain.run("stacked", body, [shape(2 * rows, width)], [tokens, cotangent])[0]

        def product(step, side):
            def body(ins, outs):
                left = [ins[0][:, pl.ds(band * width, width)] for band in range(2)]
                for piece in tiles(units, 512):
                    part = jnp.dot(left[0], ins[1][:, piece], preferred_element_type=F32)
                    part = part + jnp.dot(left[1], ins[2][:, piece], preferred_element_type=F32)
                    outs[0][:, piece] = part.astype(BF16)

            weights = (w_out_t, w_out_t_far) if side else (w_in, w_in_far)
            total, = chain.run("product", body, [shape(height(step), units)], [blocks[step][side], *weights])
            sums[side, step] = (over_chips(total), 0)

        def own_part(left, weight_ref, side, piece):
            if side == 0:
                return jnp.dot(left, weight_ref[:, piece], preferred_element_type=F32)
            return lax.dot_general(
                left, weight_ref[piece, :], (((1,), (1,)), ((), ())), preferred_element_type=F32)

        def own_other(side):
            def body(ins, outs):
                left = ins[0][half_at(1, half, side * rows), :]
                for piece in tiles(units, 512):
                    outs[0][:, piece] = own_part(left, ins[1], side, piece).astype(BF16)

            return to_sibling(
                chain.run("own_other", body, [shape(half, units)], [own, (w_in, w_out)[side]])[0])

        def own_mine(came_pre, came_dact):
            def body(ins, outs):
                for side in range(2):
                    left = ins[0][half_at(0, half, side * rows), :]
                    here = pl.ds(side * half, half)
                    for piece in tiles(units, 512):
                        part = own_part(left, ins[1 + side], side, piece)
                        outs[0][here, piece] = (part + ins[3 + side][:, piece].astype(F32)).astype(BF16)

            total, = chain.run(
                "own_mine", body, [shape(2 * half, units)], [own, w_in, w_out, came_pre, came_dact])
            parts = over_chips(total)
            sums[0, 0], sums[1, 0] = (parts, 0), (parts, half)

        def both_bands(came):
            def body(ins, outs):
                for side in range(2):
                    outs[side][:, 0:width] = ins[0][side * rows:(side + 1) * rows, :]
                    outs[side][:, width:2 * width] = ins[1][side * rows:(side + 1) * rows, :]

            return chain.run("both_bands", body, [shape(rows, 2 * width)] * 2, [own, came])

        def relay(step, side):
            def body(ins, outs):
                outs[0][...] = ins[0][...] if step + 1 < far else ins[0][half_at(0, half), :]

            size = shape(height(step + 1), 2 * width)
            blocks[step + 1][side] = outward(chain.run("relay", body, [size], [blocks[step][side]])[0])

        def gelu(step):
            parts, offset = sums[0, step]

            def body(ins, outs):
                for strip in tiles(height(step), 16):
                    value = added(ins, shifted(strip, offset))
                    cdf = 0.5 * (1.0 + lax.erf(value * 0.7071067811865476))
                    pdf = jnp.exp(-0.5 * value * value) * 0.3989422804014327
                    outs[0][strip, :] = (value * cdf).astype(BF16)
                    outs[1][strip, :] = (cdf + value * pdf).astype(BF16)

            act[step], slope[step] = chain.run("gelu", body, [shape(height(step), units)] * 2, parts)

        def slopes(step):
            parts, offset = sums[1, step]

            def body(ins, outs):
                for strip in tiles(height(step), 16):
                    outs[0][strip, :] = (added(ins[1:], shifted(strip, offset)) * ins[0][strip, :].astype(F32)).astype(BF16)

            dpre[step], = chain.run("slopes", body, [shape(height(step), units)], [slope[step]] + parts)

        def term(step, hidden, weights, came=None):
            def body(ins, outs):
                for band in range(2):
                    for piece in tiles(width, 512):
                        part = jnp.dot(ins[0][...], ins[1 + band][:, piece], preferred_element_type=F32)
                        there = pl.ds(band * width + piece.start, piece.size)
                        if came is None:
                            outs[0][:, there] = part.astype(BF16)
                        elif step + 1 < far:
                            outs[0][:, there] = (part + ins[3][:, there].astype(F32)).astype(BF16)
                        else:
                            mine = half_at(0, half)
                            outs[0][:, there] = part.astype(BF16)
                            outs[0][mine, there] = (
                                outs[0][mine, there].astype(F32) + ins[3][:, there].astype(F32)).astype(BF16)

            ins = [hidden[step], *weights] + ([] if came is None else [came])
            return chain.run("term", body, [shape(height(step), 2 * width)], ins)[0]

        def joined(step, part, came):
            def body(ins, outs):
                if step + 1 < far:
                    for strip in tiles(rows, 16):
                        outs[0][strip, :] = added(ins, strip).astype(BF16)
                else:
                    outs[0][...] = ins[0][...]
                    mine = half_at(0, half)
                    outs[0][mine, :] = (ins[0][mine, :].astype(F32) + ins[1][...].astype(F32)).astype(BF16)

            return chain.run("joined", body, [shape(rows, 2 * width)], [part, came])[0]

        def settled(part, came):
            def body(ins, outs):
                mine = half_at(0, half)
                for band in range(2):
                    there = pl.ds(band * width, width)
                    outs[band][...] = ins[1][:, there]
                    outs[band][mine, :] = (
                        ins[1][mine, there].astype(F32) + ins[0][:, there].astype(F32)).astype(BF16)

            keep, give = chain.run("settled", body, [shape(rows, width)] * 2, [part, came], False)
            return keep, to_sibling(give)

        def finish(residual, keep, came):
            def body(ins, outs):
                outs[0][...] = added(ins, slice(None)).astype(BF16)

            return chain.run("finish", body, [shape(rows, width)], [residual, keep, came], False)[0]

        def turned(weight):
            def body(ins, outs):
                for piece in tiles(weight.shape[0], 256):
                    outs[0][:, piece] = ins[0][piece, :].T

            return chain.run("turned", body, [shape(weight.shape[1], weight.shape[0])], [weight], False)[0]

        def packed_hidden(hidden, steps):
            def body(ins, outs):
                start = 0
                for ref, step in zip(ins, steps):
                    outs[0][start:start + height(step), :] = ref[...]
                    start += height(step)

            total = sum(height(step) for step in steps)
            result, = chain.run("packed", body, [shape(total, units)], [hidden[step] for step in steps], False)
            return result, to_sibling(result)

        def packed_stream():
            def body(ins, outs):
                for side in range(2):
                    start = 0
                    for ref, step in zip(ins[side::2], order):
                        size = height(step)
                        source = half_at(0, half) if step == 0 else pl.ds(0, size)
                        outs[side][start:start + size, :] = ref[source, 0:width]
                        outs[2][side * share + start:side * share + start + size, :] = ref[source, width:2 * width]
                        start += size

            outs = [shape(share, width)] * 2 + [shape(2 * share, width)]
            tok, cot, give = chain.run("packed", body, outs, [block for step in order for block in blocks[step]], False)
            return tok, cot, to_sibling(give)

        sums, act, slope, dpre, act_term = {}, {}, {}, {}, {}
        blocks = {step: [None, None] for step in range(far + 1)}
        everything = slice(None)

        own = stacked()
        own_far = to_sibling(own)
        other_pre = own_other(0)
        blocks[0] = both_bands(own_far)
        blocks[1] = [outward(block) for block in blocks[0]]
        other_dact = own_other(1)
        own_mine(other_pre, other_dact)
        w_in_t = turned(w_in)
        w_in_t_far = to_sibling(w_in_t)
        w_out_t = turned(w_out)
        w_in_far = turned(w_in_t_far)

        for step in range(1, far + 1):
            if step < far:
                relay(step, 0)
            product(step, 0)
            if step < far:
                gelu(step - 1)
                relay(step, 1)
                if step == 1:
                    slopes(0)
                    w_out_t_far = to_sibling(w_out_t)
                    w_out_far = turned(w_out_t_far)
                else:
                    act_term[step - 2] = term(step - 2, act, (w_out, w_out_far))
        product(far, 1)
        gelu(far - 1)
        act_term[far - 2] = term(far - 2, act, (w_out, w_out_far))
        act_term[far - 1] = term(far - 1, act, (w_out, w_out_far))
        gelu(far)
        going = homeward(term(far, act, (w_out, w_out_far)))
        product(far - 1, 1)
        tok_own, cot_own, stream_far = packed_stream()
        act_own, act_far = packed_hidden(act, order)
        back_going = None
        for step in range(far, 1, -1):
            slopes(step)
            going = homeward(joined(step - 1, act_term[step - 1], going))
            back_going = homeward(term(step, dpre, (w_in_t, w_in_t_far), back_going))
            if step > 2:
                product(step - 2, 1)
            if step == far:
                back_own = term(0, dpre, (w_in_t, w_in_t_far))
            if step == far - 1:
                grad_out = chain.outer("grad_out", [
                    (act_own, everything, cot_own, everything),
                    (act_far, everything, stream_far, pl.ds(share, share)),
                ])
        early_own, early_far = packed_hidden(dpre, order[:-1])
        early, late = pl.ds(0, share - rows), pl.ds(share - rows, rows)
        grad_in = chain.outer("grad_in_early", [
            (tok_own, early, early_own, everything),
            (stream_far, early, early_far, everything),
        ])
        slopes(1)
        late_own, late_far = dpre[1], to_sibling(dpre[1])
        back_going = homeward(term(1, dpre, (w_in_t, w_in_t_far), back_going))
        mixed = finish(tokens, *settled(act_term[0], going))
        block_out = lax.all_to_all(mixed, "col", split_axis=0, concat_axis=1, tiled=True)
        grad_in = chain.outer("grad_in", [
            (tok_own, late, late_own, everything),
            (stream_far, late, late_far, everything),
        ], grad_in)
        grad_tokens = finish(cotangent, *settled(back_own, back_going))
        return block_out, grad_tokens, grad_in, grad_out

    in_specs = (P("row", "col"), P("col", "row"), P("row", "col"), P("row", "col"))
    out_specs = (P(("row", "col"), None), P("row", "col"), P("col", "row"), P("row", "col"))
    return jax.shard_map(local, mesh=mesh, in_specs=in_specs, out_specs=out_specs, check_vma=False)
```

```python
import jax
import jax.numpy as jnp
from jax import lax
from jax.experimental import pallas as pl
from jax.experimental.pallas import tpu as pltpu
from jax.sharding import PartitionSpec as P

CORES = 2
F32 = jnp.float32
BF16 = jnp.bfloat16
MIB = 2 ** 20
IN_VMEM = pl.BlockSpec(memory_space=pltpu.VMEM)
ANYWHERE = pl.BlockSpec(memory_space=pl.ANY)
MICROSECOND = 10 ** 9
COSTS = {"grad_out": 6.0, "grad_in": 6.0, "grad_in_early": 6.0, "grad_out_early": 6.0, "summed": 0.3, "settled": 0.3}
USUAL_COST = 3.0


def cost(name):
    return pl.CostEstimate(
        flops=int(COSTS.get(name, USUAL_COST) * MICROSECOND), bytes_accessed=0, transcendentals=0)


def ring_order(count):
    if count % 4:
        return list(range(count))
    minor = count // 4
    order = [major * minor for major in range(4)]
    for turn, major in enumerate(reversed(range(4))):
        steps = range(1, minor) if turn % 2 == 0 else range(minor - 1, 0, -1)
        order += [major * minor + step for step in steps]
    return order


def ring_pairs(count, n_col, sign):
    order = ring_order(count)
    pairs = []
    for place in range(count):
        for col in range(n_col):
            step = sign if col % CORES == 0 else -sign
            target = order[(place + step) % count]
            pairs.append((order[place] * n_col + col, target * n_col + col))
    return pairs


def shape(rows, columns):
    return jax.ShapeDtypeStruct((rows, columns), BF16)


def half_at(which, half, base=0):
    core = lax.axis_index("col") % CORES
    return pl.ds(pl.multiple_of((core if which == 0 else 1 - core) * half + base, half), half)


def tiles(extent, size):
    return [pl.ds(start, min(size, extent - start)) for start in range(0, extent, size)]


def added(refs, strip):
    total = refs[0][strip, :].astype(F32)
    for ref in refs[1:]:
        total = total + ref[strip, :].astype(F32)
    return total


class Chain:
    def __init__(self, first):
        self.last = first

    def run(self, name, body, outs, ins, holds=True, also=()):
        behind = [self.last, *also]

        def kernel(*refs):
            body(refs[len(behind):len(behind) + len(ins)], refs[len(behind) + len(ins):])

        result = pl.pallas_call(
            kernel,
            out_shape=outs,
            in_specs=[ANYWHERE] * len(behind) + [IN_VMEM] * len(ins),
            out_specs=[IN_VMEM] * len(outs),
            compiler_params=pltpu.CompilerParams(vmem_limit_bytes=8 * MIB),
            cost_estimate=cost(name),
            name=name,
        )(*behind, *ins)
        if holds:
            self.last = result[0]
        return result

    def outer(self, name, pairs, begun=None):
        tile = min(512, pairs[0][0].shape[1])
        arrays = [array for left, _, right, _ in pairs for array in (left, right)]
        out = jax.ShapeDtypeStruct((pairs[0][0].shape[1], pairs[0][2].shape[1]), F32)
        bands = pl.BlockSpec((tile, out.shape[1]), lambda band: (band, 0))
        more = [] if begun is None else [begun]

        def kernel(after_ref, *refs):
            band = pl.ds(pl.multiple_of(pl.program_id(0) * tile, tile), tile)
            total = None if begun is None else refs[len(arrays)][...]
            for index, (_, left_rows, _, right_rows) in enumerate(pairs):
                part = lax.dot_general(
                    refs[2 * index][left_rows, band], refs[2 * index + 1][right_rows, :],
                    (((0,), (0,)), ((), ())), preferred_element_type=F32)
                total = part if total is None else total + part
            refs[-2][...] = total
            refs[-1][...] = jnp.zeros_like(refs[-1])

        result, self.last = pl.pallas_call(
            kernel,
            grid=(out.shape[0] // tile,),
            out_shape=[out, shape(16, 128)],
            in_specs=[ANYWHERE] + [IN_VMEM] * len(arrays) + [bands] * len(more),
            out_specs=[bands, IN_VMEM],
            compiler_params=pltpu.CompilerParams(vmem_limit_bytes=24 * MIB),
            cost_estimate=cost(name),
            name=name,
        )(self.last, *arrays, *more)
        return result


def solution(mesh):
    n_row, n_col = mesh.shape["row"], mesh.shape["col"]
    n_x = n_col // CORES
    far = n_row // 2
    out_ring = ring_pairs(n_row, n_col, 1)
    back_ring = ring_pairs(n_row, n_col, -1)
    sibling = [(col, col ^ 1) for col in range(n_col)]
    chip_ring = [(col, (col + CORES) % n_col) for col in range(n_col)]

    def outward(value):
        return lax.ppermute(value, ("row", "col"), out_ring)

    def homeward(value):
        return lax.ppermute(value, ("row", "col"), back_ring)

    def to_sibling(value):
        return lax.ppermute(value, "col", sibling)

    def over_chips(value):
        parts = [value]
        for _ in range(n_x - 1):
            parts.append(lax.ppermute(parts[-1], "col", chip_ring))
        return parts

    def local(tokens, w_in, w_out, cotangent):
        rows, width = tokens.shape
        half = rows // 2
        units = w_in.shape[1]
        chain = Chain(tokens)
        order = list(range(far, -1, -1))

        def height(step):
            return rows if 0 < step < far else half

        share = sum(height(step) for step in order)

        def product(step, side):
            def body(ins, outs):
                left = [ins[0][half_at(0, half) if step == 0 else slice(None), pl.ds(band * width, width)]
                        for band in range(2)]
                for piece in tiles(units, 512):
                    part = jnp.dot(left[0], ins[1][:, piece], preferred_element_type=F32)
                    part = part + jnp.dot(left[1], ins[2][:, piece], preferred_element_type=F32)
                    outs[0][:, piece] = part.astype(BF16)

            weights = (w_out_t, w_out_t_far) if side else (w_in, w_in_far)
            total, = chain.run("product", body, [shape(height(step), units)], [blocks[step][side], *weights])
            sums[side, step] = over_chips(total)

        def own_other():
            def body(ins, outs):
                left = ins[0][half_at(1, half), :]
                for piece in tiles(units, 512):
                    outs[0][:, piece] = jnp.dot(left, ins[1][:, piece], preferred_element_type=F32).astype(BF16)

            return to_sibling(chain.run("own_other", body, [shape(half, units)], [tokens, w_in])[0])

        def own_mine(came):
            def body(ins, outs):
                left = ins[0][half_at(0, half), :]
                for piece in tiles(units, 512):
                    part = jnp.dot(left, ins[1][:, piece], preferred_element_type=F32)
                    outs[0][:, piece] = (part + ins[2][:, piece].astype(F32)).astype(BF16)

            total, = chain.run("own_mine", body, [shape(half, units)], [tokens, w_in, came])
            sums[0, 0] = over_chips(total)

        def both_bands(came):
            def body(ins, outs):
                for side in range(2):
                    outs[side][:, 0:width] = ins[side][...]
                    outs[side][:, width:2 * width] = ins[2 + side][...]

            return chain.run("both_bands", body, [shape(rows, 2 * width)] * 2, [tokens, cotangent, *came])

        def held(weights):
            def body(ins, outs):
                for ref, out in zip(ins, outs):
                    for piece in tiles(ref.shape[0], 256):
                        out[piece, :] = ref[piece, :]

            return chain.run("held", body, [shape(*weight.shape) for weight in weights], weights, False)

        def relay(step, side):
            def body(ins, outs):
                outs[0][...] = ins[0][...] if step + 1 < far else ins[0][half_at(0, half), :]

            size = shape(height(step + 1), 2 * width)
            blocks[step + 1][side] = outward(chain.run("relay", body, [size], [blocks[step][side]])[0])

        def gelu_of(value):
            cdf = 0.5 * (1.0 + lax.erf(value * 0.7071067811865476))
            pdf = jnp.exp(-0.5 * value * value) * 0.3989422804014327
            return value * cdf, cdf + value * pdf

        def gelu(step, also=()):
            def body(ins, outs):
                for strip in tiles(height(step), 16):
                    act_rows, slope_rows = gelu_of(added(ins, strip))
                    outs[0][strip, :] = act_rows.astype(BF16)
                    outs[1][strip, :] = slope_rows.astype(BF16)

            act[step], slope[step] = chain.run(
                "gelu", body, [shape(height(step), units)] * 2, sums[0, step], True, also)
            act_far[step] = to_sibling(act[step])

        def slopes(step, also=()):
            def body(ins, outs):
                for strip in tiles(height(step), 16):
                    value = added(ins[1:], strip) * ins[0][strip, :].astype(F32)
                    outs[0][strip, :] = value.astype(BF16)

            dpre[step], = chain.run(
                "slopes", body, [shape(height(step), units)], [slope[step]] + sums[1, step], True, also)
            dpre_far[step] = to_sibling(dpre[step])

        def term(step, hidden, weights, came=None):
            def body(ins, outs):
                for band in range(2):
                    for piece in tiles(width, 512):
                        part = jnp.dot(ins[0][...], ins[1 + band][:, piece], preferred_element_type=F32)
                        there = pl.ds(band * width + piece.start, piece.size)
                        if came is None:
                            outs[0][:, there] = part.astype(BF16)
                        elif step + 1 < far:
                            outs[0][:, there] = (part + ins[3][:, there].astype(F32)).astype(BF16)
                        else:
                            mine = half_at(0, half)
                            outs[0][:, there] = part.astype(BF16)
                            outs[0][mine, there] = (
                                outs[0][mine, there].astype(F32) + ins[3][:, there].astype(F32)).astype(BF16)

            ins = [hidden[step], *weights] + ([] if came is None else [came])
            return chain.run("term", body, [shape(height(step), 2 * width)], ins)[0]

        def joined(step, part, came):
            def body(ins, outs):
                if step + 1 < far:
                    for strip in tiles(rows, 16):
                        outs[0][strip, :] = added(ins, strip).astype(BF16)
                else:
                    outs[0][...] = ins[0][...]
                    mine = half_at(0, half)
                    outs[0][mine, :] = (ins[0][mine, :].astype(F32) + ins[1][...].astype(F32)).astype(BF16)

            return chain.run("joined", body, [shape(rows, 2 * width)], [part, came])[0]

        def settled(part, came):
            def body(ins, outs):
                mine = half_at(0, half)
                for band in range(2):
                    there = pl.ds(band * width, width)
                    outs[band][...] = ins[1][:, there]
                    outs[band][mine, :] = (
                        ins[1][mine, there].astype(F32) + ins[0][:, there].astype(F32)).astype(BF16)

            keep, give = chain.run("settled", body, [shape(rows, width)] * 2, [part, came])
            return keep, to_sibling(give)

        def finish(residual, keep, came):
            def body(ins, outs):
                outs[0][...] = added(ins, slice(None)).astype(BF16)

            return chain.run("finish", body, [shape(rows, width)], [residual, keep, came], False)[0]

        piece = rows // n_col

        def halved(part, came):
            def body(ins, outs):
                core = lax.axis_index("col") % CORES
                low = ins[0][...].astype(F32)
                zero = jnp.zeros_like(low)
                total = ins[1][...].astype(F32) + jnp.concatenate(
                    [jnp.where(core == 0, low, zero), jnp.where(core == 0, zero, low)])
                total = total.astype(BF16)
                for chip in range(n_x):
                    first, second = (
                        total[(2 * chip + index) * piece:(2 * chip + index + 1) * piece] for index in range(2))
                    outs[0][chip * piece:(chip + 1) * piece, :] = jnp.where(core == 0, first, second)
                    given = jnp.where(core == 0, second, first)
                    outs[1][chip * piece:(chip + 1) * piece, 0:width] = given[:, width:2 * width]
                    outs[1][chip * piece:(chip + 1) * piece, width:2 * width] = given[:, 0:width]

            keep, give = chain.run("halved", body, [shape(half, 2 * width)] * 2, [part, came])
            return keep, to_sibling(give)

        def spread(keep, other):
            def summed(ins, outs):
                col = lax.axis_index("col")
                core, here = col % CORES, col // CORES
                for offset in range(n_x):
                    chip = (here + offset) % n_x
                    there = pl.ds(pl.multiple_of(chip * piece, piece), piece)
                    stream = pl.ds(pl.multiple_of((chip * CORES + core) * piece, piece), piece)
                    outs[offset][...] = added(
                        [ins[0].at[there], ins[1].at[there], ins[2].at[stream]], slice(None)).astype(BF16)

            sent = chain.run(
                "summed", summed, [shape(piece, 2 * width)] * n_x, [keep, other, blocks[0][0]])
            bands = [sent[0]]
            for offset in range(1, n_x):
                pairs = [(col, (col + CORES * offset) % n_col) for col in range(n_col)]
                bands.append(lax.ppermute(sent[offset], "col", pairs))

            def laid(ins, outs):
                col = lax.axis_index("col")
                core, here = col % CORES, col // CORES
                for offset in range(n_x):
                    chip = (here - offset + n_x) % n_x
                    for band in range(CORES):
                        start = (chip * CORES + (core + band) % CORES) * width
                        outs[0][:, pl.ds(pl.multiple_of(start, width), width)] = ins[offset][
                            :, band * width:(band + 1) * width]

            return chain.run("laid", laid, [shape(piece, n_col * width)], bands, False)[0]

        def turned(weight):
            def body(ins, outs):
                for piece in tiles(weight.shape[0], 256):
                    outs[0][:, piece] = ins[0][piece, :].T

            return chain.run("turned", body, [shape(weight.shape[1], weight.shape[0])], [weight])[0]

        def packed_hidden(hidden, steps):
            def body(ins, outs):
                start = 0
                for ref, step in zip(ins, steps):
                    outs[0][start:start + height(step), :] = ref[...]
                    start += height(step)

            total = sum(height(step) for step in steps)
            return chain.run("packed", body, [shape(total, units)], [hidden[step] for step in steps], False)[0]

        def packed_stream():
            def body(ins, outs):
                for side in range(2):
                    start = 0
                    for ref, step in zip(ins[side::2], order):
                        size = height(step)
                        source = half_at(0, half) if step == 0 else pl.ds(0, size)
                        outs[side][start:start + size, :] = ref[source, 0:width]
                        outs[2][side * share + start:side * share + start + size, :] = ref[source, width:2 * width]
                        start += size

            outs = [shape(share, width)] * 2 + [shape(2 * share, width)]
            tok, cot, give = chain.run("packed", body, outs, [block for step in order for block in blocks[step]], False)
            return tok, cot, to_sibling(give)

        sums, act, slope, dpre, act_term, act_far, dpre_far = {}, {}, {}, {}, {}, {}, {}
        blocks = {step: [None, None] for step in range(far + 1)}
        everything = slice(None)

        stream = [to_sibling(tokens), to_sibling(cotangent)]
        came = own_other()
        blocks[0] = both_bands(stream)
        blocks[1] = [outward(block) for block in blocks[0]]
        own_mine(came)
        w_in_far, w_out_far = (to_sibling(weight) for weight in held([w_in, w_out]))

        for step in range(1, far + 1):
            if step < far:
                relay(step, 0)
            product(step, 0)
            if step < far:
                gelu(step - 1, [act_far[step - 2]] if step > 1 else [])
                relay(step, 1)
            if step == 1:
                w_in_t, w_in_t_far = turned(w_in), turned(w_in_far)
            if step == 2:
                w_out_t, w_out_t_far = turned(w_out), turned(w_out_far)
            elif 2 < step < far:
                act_term[step - 3] = term(step - 3, act, (w_out, w_out_far))
        product(far, 1)
        act_term[max(far - 3, 0)] = term(max(far - 3, 0), act, (w_out, w_out_far))
        gelu(far - 1, [act_far[far - 2]])
        tok_own, cot_own, stream_far = packed_stream()
        for step in range(max(far - 3, 0) + 1, far):
            act_term[step] = term(step, act, (w_out, w_out_far))
        gelu(far, [act_far[far - 1], stream_far])
        going = homeward(term(far, act, (w_out, w_out_far)))
        product(far - 1, 1)
        back_going = None
        for step in range(far, 1, -1):
            slopes(step, [act_far[far] if step == far else dpre_far[step + 1]])
            back_going = homeward(term(step, dpre, (w_in_t, w_in_t_far), back_going))
            going = homeward(joined(step - 1, act_term[step - 1], going))
            product(step - 2, 1)
            if step == far:
                grad_out = chain.outer("grad_out_early", [
                    (packed_hidden(act, order), everything, cot_own, everything)])
            if step == far - 1:
                grad_out = chain.outer("grad_out", [
                    (packed_hidden(act_far, order), everything, stream_far, pl.ds(share, share))], grad_out)
        early, late = pl.ds(0, share - rows - half), pl.ds(share - rows - half, rows + half)
        grad_in = chain.outer("grad_in_early", [
            (tok_own, early, packed_hidden(dpre, order[:-2]), everything),
        ])
        slopes(1, [dpre_far[2]])
        back_going = homeward(term(1, dpre, (w_in_t, w_in_t_far), back_going))
        row_shares = halved(act_term[0], going)
        slopes(0)
        back_own = term(0, dpre, (w_in_t, w_in_t_far))
        block_out = spread(*row_shares)
        keep, came = settled(back_own, back_going)
        grad_in = chain.outer("grad_in", [
            (tok_own, late, packed_hidden(dpre, [1, 0]), everything),
            (stream_far, pl.ds(0, share), packed_hidden(dpre_far, order), everything),
        ], grad_in)
        grad_tokens = finish(cotangent, keep, came)
        return block_out, grad_tokens, grad_in, grad_out

    in_specs = (P("row", "col"), P("col", "row"), P("row", "col"), P("row", "col"))
    out_specs = (P(("row", "col"), None), P("row", "col"), P("col", "row"), P("row", "col"))
    return jax.shard_map(local, mesh=mesh, in_specs=in_specs, out_specs=out_specs, check_vma=False)
```

```python
import jax
import jax.numpy as jnp
from jax import lax
from jax.experimental import pallas as pl
from jax.experimental.pallas import tpu as pltpu
from jax.sharding import PartitionSpec as P

CORES = 2
F32 = jnp.float32
BF16 = jnp.bfloat16
MIB = 2 ** 20
IN_VMEM = pl.BlockSpec(memory_space=pltpu.VMEM)
IN_HBM = pl.BlockSpec(memory_space=pltpu.HBM)
ANYWHERE = pl.BlockSpec(memory_space=pl.ANY)
MICROSECOND = 10 ** 9
COSTS = {"grad_out": 6.0, "grad_in": 6.0, "grad_in_early": 6.0, "grad_out_early": 6.0, "summed": 0.3, "settled": 0.3}
USUAL_COST = 3.0


def cost(name):
    return pl.CostEstimate(
        flops=int(COSTS.get(name, USUAL_COST) * MICROSECOND), bytes_accessed=0, transcendentals=0)


def ring_order(count):
    if count % 4:
        return list(range(count))
    minor = count // 4
    order = [major * minor for major in range(4)]
    for turn, major in enumerate(reversed(range(4))):
        steps = range(1, minor) if turn % 2 == 0 else range(minor - 1, 0, -1)
        order += [major * minor + step for step in steps]
    return order


def ring_pairs(count, n_col, sign):
    order = ring_order(count)
    pairs = []
    for place in range(count):
        for col in range(n_col):
            step = sign if col % CORES == 0 else -sign
            target = order[(place + step) % count]
            pairs.append((order[place] * n_col + col, target * n_col + col))
    return pairs


def shape(rows, columns):
    return jax.ShapeDtypeStruct((rows, columns), BF16)


def half_at(which, half, base=0):
    core = lax.axis_index("col") % CORES
    return pl.ds(pl.multiple_of((core if which == 0 else 1 - core) * half + base, half), half)


def tiles(extent, size):
    return [pl.ds(start, min(size, extent - start)) for start in range(0, extent, size)]


def added(refs, strip):
    total = refs[0][strip, :].astype(F32)
    for ref in refs[1:]:
        total = total + ref[strip, :].astype(F32)
    return total


class Chain:
    def __init__(self, first):
        self.last = first

    def run(self, name, body, outs, ins, holds=True, also=(), in_spec=IN_VMEM, scratch=(), room=6):
        behind = [*([] if self.last is None else [self.last]), *also]

        def kernel(*refs):
            body(refs[len(behind):len(behind) + len(ins)], refs[len(behind) + len(ins):])

        result = pl.pallas_call(
            kernel,
            out_shape=outs,
            in_specs=[ANYWHERE] * len(behind) + [in_spec] * len(ins),
            out_specs=[IN_VMEM] * len(outs),
            scratch_shapes=list(scratch),
            compiler_params=pltpu.CompilerParams(vmem_limit_bytes=room * MIB),
            cost_estimate=cost(name),
            name=name,
        )(*behind, *ins)
        if holds:
            self.last = result[0]
        return result

    def outer(self, name, pairs, begun=None, part=(0, 1)):
        arrays = [array for left, _, right, _ in pairs for array in (left, right)]
        out = jax.ShapeDtypeStruct((pairs[0][0].shape[1], pairs[0][2].shape[1]), F32)
        tile = min(MIB // 2 // out.shape[1], out.shape[0] // part[1])
        steps = out.shape[0] // tile // part[1]
        first = part[0] * steps
        bands = pl.BlockSpec((tile, out.shape[1]), lambda band: (band + first, 0))
        more = [] if begun is None else [begun]

        def kernel(after_ref, *refs):
            band = pl.ds(pl.multiple_of((pl.program_id(0) + first) * tile, tile), tile)
            total = None if begun is None else refs[len(arrays)][...]
            for index, (_, left_rows, _, right_rows) in enumerate(pairs):
                product = lax.dot_general(
                    refs[2 * index][left_rows, band], refs[2 * index + 1][right_rows, :],
                    (((0,), (0,)), ((), ())), preferred_element_type=F32)
                total = product if total is None else total + product
            refs[-2][...] = total
            refs[-1][...] = jnp.zeros_like(refs[-1])

        result, self.last = pl.pallas_call(
            kernel,
            grid=(steps,),
            out_shape=[out, shape(16, 128)],
            in_specs=[ANYWHERE] + [IN_VMEM] * len(arrays) + [bands] * len(more),
            out_specs=[bands, IN_VMEM],
            input_output_aliases={1 + len(arrays): 0} if more else {},
            compiler_params=pltpu.CompilerParams(vmem_limit_bytes=16 * MIB),
            cost_estimate=cost(name),
            name=name,
        )(self.last, *arrays, *more)
        return result


def solution(mesh):
    n_row, n_col = mesh.shape["row"], mesh.shape["col"]
    n_x = n_col // CORES
    far = n_row // 2
    out_ring = ring_pairs(n_row, n_col, 1)
    back_ring = ring_pairs(n_row, n_col, -1)
    sibling = [(col, col ^ 1) for col in range(n_col)]
    chip_ring = [(col, (col + CORES) % n_col) for col in range(n_col)]

    def outward(value):
        return lax.ppermute(value, ("row", "col"), out_ring)

    def homeward(value):
        return lax.ppermute(value, ("row", "col"), back_ring)

    def to_sibling(value):
        return lax.ppermute(value, "col", sibling)

    def over_chips(value):
        parts = [value]
        for _ in range(n_x - 1):
            parts.append(lax.ppermute(parts[-1], "col", chip_ring))
        return parts

    def local(tokens_given, w_in_given, w_out_given, cotangent_given):
        tokens, w_in, w_out, cotangent = tokens_given, w_in_given, w_out_given, cotangent_given
        rows, width = tokens.shape
        half = rows // 2
        units = w_in.shape[1]
        chain = Chain(None)
        order = list(range(far, -1, -1))

        def height(step):
            return rows if 0 < step < far else half

        share = sum(height(step) for step in order)

        def product(step, side):
            def body(ins, outs):
                left = [ins[0][half_at(0, half) if step == 0 else slice(None), pl.ds(band * width, width)]
                        for band in range(2)]
                for piece in tiles(units, 512):
                    part = jnp.dot(left[0], ins[1][:, piece], preferred_element_type=F32)
                    part = part + jnp.dot(left[1], ins[2][:, piece], preferred_element_type=F32)
                    outs[0][:, piece] = part.astype(BF16)

            weights = (w_out_t, w_out_t_far) if side else (w_in, w_in_far)
            total, = chain.run("product", body, [shape(height(step), units)], [blocks[step][side], *weights])
            sums[side, step] = over_chips(total)

        def begun():
            cuts = tiles(units, units // 4)

            def body(ins, outs):
                held_tokens, held_cotangent, held_in, held_out, product = outs[:5]
                copies = [pltpu.make_async_copy(ins[0], held_tokens, outs[5].at[0])]
                for index, piece in enumerate(cuts):
                    copies.append(pltpu.make_async_copy(
                        ins[2].at[:, piece], held_in.at[:, piece], outs[5].at[1 + index]))
                copies.append(pltpu.make_async_copy(ins[1], held_cotangent, outs[5].at[5]))
                copies.append(pltpu.make_async_copy(ins[3], held_out, outs[5].at[6]))
                for copy in copies:
                    copy.start()
                copies[0].wait()
                left = held_tokens[half_at(1, half), :]
                for index, piece in enumerate(cuts):
                    copies[1 + index].wait()
                    product[:, piece] = jnp.dot(
                        left, held_in[:, piece], preferred_element_type=F32).astype(BF16)
                copies[5].wait()
                copies[6].wait()

            arrays = [tokens, cotangent, w_in, w_out]
            return chain.run(
                "begun", body, [shape(*array.shape) for array in arrays] + [shape(half, units)], arrays,
                in_spec=IN_HBM, scratch=[pltpu.SemaphoreType.DMA((7,))], room=43)

        def own_mine(came):
            def body(ins, outs):
                left = ins[0][half_at(0, half), :]
                for piece in tiles(units, 512):
                    part = jnp.dot(left, ins[1][:, piece], preferred_element_type=F32)
                    outs[0][:, piece] = (part + ins[2][:, piece].astype(F32)).astype(BF16)

            total, = chain.run("own_mine", body, [shape(half, units)], [tokens, w_in, came])
            sums[0, 0] = over_chips(total)

        def both_bands(came):
            def body(ins, outs):
                for side in range(2):
                    outs[side][:, 0:width] = ins[side][...]
                    outs[side][:, width:2 * width] = ins[2 + side][...]

            return chain.run("both_bands", body, [shape(rows, 2 * width)] * 2, [tokens, cotangent, *came])

        def held(weights, came):
            return pl.pallas_call(
                lambda *refs: None,
                out_shape=[shape(*weight.shape) for weight in weights],
                in_specs=[ANYWHERE] * (2 + len(came)),
                out_specs=[ANYWHERE] * 2,
                input_output_aliases={0: 0, 1: 1},
                cost_estimate=cost("held"),
                name="held",
            )(*weights, *came)

        def relay(step, side):
            def body(ins, outs):
                outs[0][...] = ins[0][...] if step + 1 < far else ins[0][half_at(0, half), :]

            size = shape(height(step + 1), 2 * width)
            blocks[step + 1][side] = outward(chain.run("relay", body, [size], [blocks[step][side]])[0])

        def gelu_of(value):
            cdf = 0.5 * (1.0 + lax.erf(value * 0.7071067811865476))
            pdf = jnp.exp(-0.5 * value * value) * 0.3989422804014327
            return value * cdf, cdf + value * pdf

        def gelu(step, also=()):
            def body(ins, outs):
                for strip in tiles(height(step), 16):
                    act_rows, slope_rows = gelu_of(added(ins, strip))
                    outs[0][strip, :] = act_rows.astype(BF16)
                    outs[1][strip, :] = slope_rows.astype(BF16)

            act[step], slope[step] = chain.run(
                "gelu", body, [shape(height(step), units)] * 2, sums[0, step], True, also)
            act_far[step] = to_sibling(act[step])

        def slopes(step, also=()):
            def body(ins, outs):
                for strip in tiles(height(step), 16):
                    value = added(ins[1:], strip) * ins[0][strip, :].astype(F32)
                    outs[0][strip, :] = value.astype(BF16)

            dpre[step], = chain.run(
                "slopes", body, [shape(height(step), units)], [slope[step]] + sums[1, step], True, also)
            dpre_far[step] = to_sibling(dpre[step])

        def term(step, hidden, weights, came=None):
            def body(ins, outs):
                for band in range(2):
                    for piece in tiles(width, 512):
                        part = jnp.dot(ins[0][...], ins[1 + band][:, piece], preferred_element_type=F32)
                        there = pl.ds(band * width + piece.start, piece.size)
                        if came is None:
                            outs[0][:, there] = part.astype(BF16)
                        elif step + 1 < far:
                            outs[0][:, there] = (part + ins[3][:, there].astype(F32)).astype(BF16)
                        else:
                            mine = half_at(0, half)
                            outs[0][:, there] = part.astype(BF16)
                            outs[0][mine, there] = (
                                outs[0][mine, there].astype(F32) + ins[3][:, there].astype(F32)).astype(BF16)

            ins = [hidden[step], *weights] + ([] if came is None else [came])
            return chain.run("term", body, [shape(height(step), 2 * width)], ins)[0]

        def joined(step, part, came):
            def body(ins, outs):
                if step + 1 < far:
                    for strip in tiles(rows, 16):
                        outs[0][strip, :] = added(ins, strip).astype(BF16)
                else:
                    outs[0][...] = ins[0][...]
                    mine = half_at(0, half)
                    outs[0][mine, :] = (ins[0][mine, :].astype(F32) + ins[1][...].astype(F32)).astype(BF16)

            return chain.run("joined", body, [shape(rows, 2 * width)], [part, came])[0]

        def settled(part, came):
            def body(ins, outs):
                mine = half_at(0, half)
                for band in range(2):
                    there = pl.ds(band * width, width)
                    outs[band][...] = ins[1][:, there]
                    outs[band][mine, :] = (
                        ins[1][mine, there].astype(F32) + ins[0][:, there].astype(F32)).astype(BF16)

            keep, give = chain.run("settled", body, [shape(rows, width)] * 2, [part, came])
            return keep, to_sibling(give)

        def finish(residual, keep, came):
            def body(ins, outs):
                outs[0][...] = added(ins, slice(None)).astype(BF16)

            return chain.run("finish", body, [shape(rows, width)], [residual, keep, came], False)[0]

        piece = rows // n_col

        def halved(part, came):
            def body(ins, outs):
                core = lax.axis_index("col") % CORES
                low = ins[0][...].astype(F32)
                zero = jnp.zeros_like(low)
                total = ins[1][...].astype(F32) + jnp.concatenate(
                    [jnp.where(core == 0, low, zero), jnp.where(core == 0, zero, low)])
                total = total.astype(BF16)
                for chip in range(n_x):
                    first, second = (
                        total[(2 * chip + index) * piece:(2 * chip + index + 1) * piece] for index in range(2))
                    outs[0][chip * piece:(chip + 1) * piece, :] = jnp.where(core == 0, first, second)
                    given = jnp.where(core == 0, second, first)
                    outs[1][chip * piece:(chip + 1) * piece, 0:width] = given[:, width:2 * width]
                    outs[1][chip * piece:(chip + 1) * piece, width:2 * width] = given[:, 0:width]

            keep, give = chain.run("halved", body, [shape(half, 2 * width)] * 2, [part, came])
            return keep, to_sibling(give)

        def spread(keep, other):
            def summed(ins, outs):
                col = lax.axis_index("col")
                core, here = col % CORES, col // CORES
                for offset in range(n_x):
                    chip = (here + offset) % n_x
                    there = pl.ds(pl.multiple_of(chip * piece, piece), piece)
                    stream = pl.ds(pl.multiple_of((chip * CORES + core) * piece, piece), piece)
                    outs[offset][...] = added(
                        [ins[0].at[there], ins[1].at[there], ins[2].at[stream]], slice(None)).astype(BF16)

            sent = chain.run(
                "summed", summed, [shape(piece, 2 * width)] * n_x, [keep, other, blocks[0][0]])
            bands = [sent[0]]
            for offset in range(1, n_x):
                pairs = [(col, (col + CORES * offset) % n_col) for col in range(n_col)]
                bands.append(lax.ppermute(sent[offset], "col", pairs))

            def laid(ins, outs):
                col = lax.axis_index("col")
                core, here = col % CORES, col // CORES
                for offset in range(n_x):
                    chip = (here - offset + n_x) % n_x
                    for band in range(CORES):
                        start = (chip * CORES + (core + band) % CORES) * width
                        outs[0][:, pl.ds(pl.multiple_of(start, width), width)] = ins[offset][
                            :, band * width:(band + 1) * width]

            return chain.run("laid", laid, [shape(piece, n_col * width)], bands, False)[0]

        def turned(weight):
            def body(ins, outs):
                for piece in tiles(weight.shape[0], 256):
                    outs[0][:, piece] = ins[0][piece, :].T

            return chain.run("turned", body, [shape(weight.shape[1], weight.shape[0])], [weight])[0]

        def packed_hidden(hidden, steps):
            def body(ins, outs):
                start = 0
                for ref, step in zip(ins, steps):
                    outs[0][start:start + height(step), :] = ref[...]
                    start += height(step)

            total = sum(height(step) for step in steps)
            return chain.run("packed", body, [shape(total, units)], [hidden[step] for step in steps], False)[0]

        def packed_stream():
            def body(ins, outs):
                for side in range(2):
                    start = 0
                    for ref, step in zip(ins[side::2], order):
                        size = height(step)
                        source = half_at(0, half) if step == 0 else pl.ds(0, size)
                        outs[side][start:start + size, :] = ref[source, 0:width]
                        outs[2][side * share + start:side * share + start + size, :] = ref[source, width:2 * width]
                        start += size

            outs = [shape(share, width)] * 2 + [shape(2 * share, width)]
            tok, cot, give = chain.run("packed", body, outs, [block for step in order for block in blocks[step]], False)
            return tok, cot, to_sibling(give)

        sums, act, slope, dpre, act_term, act_far, dpre_far = {}, {}, {}, {}, {}, {}, {}
        blocks = {step: [None, None] for step in range(far + 1)}
        everything = slice(None)

        stream = [to_sibling(tokens_given), to_sibling(cotangent_given)]
        tokens, cotangent, w_in, w_out, given = begun()
        came = to_sibling(given)
        w_in, w_out = held([w_in, w_out], [came, *stream])
        w_in_far, w_out_far = to_sibling(w_in), to_sibling(w_out)
        blocks[0] = both_bands(stream)
        blocks[1] = [outward(block) for block in blocks[0]]
        own_mine(came)

        for step in range(1, far + 1):
            if step < far:
                relay(step, 0)
            product(step, 0)
            if step < far:
                gelu(step - 1, [act_far[step - 2]] if step > 1 else [])
                relay(step, 1)
            if step == 1:
                w_in_t, w_in_t_far = turned(w_in), turned(w_in_far)
            if step == 2:
                w_out_t, w_out_t_far = turned(w_out), turned(w_out_far)
            elif 2 < step < far:
                act_term[step - 3] = term(step - 3, act, (w_out, w_out_far))
        product(far, 1)
        act_term[max(far - 3, 0)] = term(max(far - 3, 0), act, (w_out, w_out_far))
        gelu(far - 1, [act_far[far - 2]])
        tok_own, cot_own, stream_far = packed_stream()
        for step in range(max(far - 3, 0) + 1, far):
            act_term[step] = term(step, act, (w_out, w_out_far))
        product(far - 1, 1)
        gelu(far, [act_far[far - 1], stream_far])
        going = homeward(term(far, act, (w_out, w_out_far)))
        back_going = None
        for step in range(far, 1, -1):
            slopes(step, [act_far[far] if step == far else dpre_far[step + 1]])
            back_going = homeward(term(step, dpre, (w_in_t, w_in_t_far), back_going))
            going = homeward(joined(step - 1, act_term[step - 1], going))
            product(step - 2, 1)
            if step == far:
                grad_out = chain.outer("grad_out_early", [
                    (packed_hidden(act, order), everything, cot_own, everything)])
            if far - 2 <= step < far:
                grad_out = chain.outer("grad_out", [
                    (packed_hidden(act_far, order), everything, stream_far, pl.ds(share, share))],
                    grad_out, (far - 1 - step, 2))
        slopes(1, [dpre_far[2]])
        back_going = homeward(term(1, dpre, (w_in_t, w_in_t_far), back_going))
        row_shares = halved(act_term[0], going)
        slopes(0)
        back_own = term(0, dpre, (w_in_t, w_in_t_far))
        block_out = spread(*row_shares)
        keep, came = settled(back_own, back_going)
        grad_in = chain.outer("grad_in", [
            (tok_own, everything, packed_hidden(dpre, order), everything),
            (stream_far, pl.ds(0, share), packed_hidden(dpre_far, order), everything),
        ])
        grad_tokens = finish(cotangent_given, keep, came)
        return block_out, grad_tokens, grad_in, grad_out

    in_specs = (P("row", "col"), P("col", "row"), P("row", "col"), P("row", "col"))
    out_specs = (P(("row", "col"), None), P("row", "col"), P("col", "row"), P("row", "col"))
    return jax.shard_map(local, mesh=mesh, in_specs=in_specs, out_specs=out_specs, check_vma=False)
```

```python
import jax
import jax.numpy as jnp
from jax import lax
from jax.experimental import pallas as pl
from jax.experimental.pallas import tpu as pltpu
from jax.sharding import PartitionSpec as P

CORES = 2
F32 = jnp.float32
BF16 = jnp.bfloat16
MIB = 2 ** 20
IN_VMEM = pl.BlockSpec(memory_space=pltpu.VMEM)
ANYWHERE = pl.BlockSpec(memory_space=pl.ANY)
MICROSECOND = 10 ** 9
COSTS = {"grad_out": 6.0, "grad_in": 0.1, "laid": 0.1, "grad_in_early": 6.0, "grad_out_early": 6.0, "summed": 0.3, "settled": 0.3}
USUAL_COST = 3.0


def cost(name):
    return pl.CostEstimate(
        flops=int(COSTS.get(name, USUAL_COST) * MICROSECOND), bytes_accessed=0, transcendentals=0)


def ring_order(count):
    if count % 4:
        return list(range(count))
    minor = count // 4
    order = [major * minor for major in range(4)]
    for turn, major in enumerate(reversed(range(4))):
        steps = range(1, minor) if turn % 2 == 0 else range(minor - 1, 0, -1)
        order += [major * minor + step for step in steps]
    return order


def ring_pairs(count, n_col, sign):
    order = ring_order(count)
    pairs = []
    for place in range(count):
        for col in range(n_col):
            step = sign if col % CORES == 0 else -sign
            target = order[(place + step) % count]
            pairs.append((order[place] * n_col + col, target * n_col + col))
    return pairs


def shape(rows, columns):
    return jax.ShapeDtypeStruct((rows, columns), BF16)


def half_at(which, half, base=0):
    core = lax.axis_index("col") % CORES
    return pl.ds(pl.multiple_of((core if which == 0 else 1 - core) * half + base, half), half)


def tiles(extent, size):
    return [pl.ds(start, min(size, extent - start)) for start in range(0, extent, size)]


def added(refs, strip):
    total = refs[0][strip, :].astype(F32)
    for ref in refs[1:]:
        total = total + ref[strip, :].astype(F32)
    return total


class Chain:
    def __init__(self, first):
        self.last = first

    def run(self, name, body, outs, ins, holds=True, also=()):
        behind = [*([] if self.last is None else [self.last]), *also]

        def kernel(*refs):
            body(refs[len(behind):len(behind) + len(ins)], refs[len(behind) + len(ins):])

        result = pl.pallas_call(
            kernel,
            out_shape=outs,
            in_specs=[ANYWHERE] * len(behind) + [IN_VMEM] * len(ins),
            out_specs=[IN_VMEM] * len(outs),
            compiler_params=pltpu.CompilerParams(vmem_limit_bytes=6 * MIB),
            cost_estimate=cost(name),
            name=name,
        )(*behind, *ins)
        if holds:
            self.last = result[0]
        return result

    def outer(self, name, pairs, begun=None, part=(0, 1)):
        arrays = [array for left, _, right, _ in pairs for array in (left, right)]
        out = jax.ShapeDtypeStruct((pairs[0][0].shape[1], pairs[0][2].shape[1]), F32)
        tile = min(512, out.shape[0] // part[1])
        steps = out.shape[0] // tile // part[1]
        first = part[0] * steps
        bands = pl.BlockSpec((tile, out.shape[1]), lambda band: (band + first, 0))
        more = [] if begun is None else [begun]

        def kernel(after_ref, *refs):
            band = pl.ds(pl.multiple_of((pl.program_id(0) + first) * tile, tile), tile)
            total = None
            for index, (_, left_rows, _, right_rows) in enumerate(pairs):
                product = lax.dot_general(
                    refs[2 * index][left_rows, band], refs[2 * index + 1][right_rows, :],
                    (((0,), (0,)), ((), ())), preferred_element_type=F32)
                total = product if total is None else total + product
            refs[-2][...] = total
            refs[-1][...] = jnp.zeros_like(refs[-1])

        result, self.last = pl.pallas_call(
            kernel,
            grid=(steps,),
            out_shape=[out, shape(16, 128)],
            in_specs=[ANYWHERE] + [IN_VMEM] * len(arrays) + [ANYWHERE] * len(more),
            out_specs=[bands, IN_VMEM],
            input_output_aliases={1 + len(arrays): 0} if more else {},
            compiler_params=pltpu.CompilerParams(vmem_limit_bytes=(14 if out.shape[1] <= 1024 else 24) * MIB),
            cost_estimate=cost(name),
            name=name,
        )(self.last, *arrays, *more)
        return result


def solution(mesh):
    n_row, n_col = mesh.shape["row"], mesh.shape["col"]
    n_x = n_col // CORES
    far = n_row // 2
    out_ring = ring_pairs(n_row, n_col, 1)
    back_ring = ring_pairs(n_row, n_col, -1)
    sibling = [(col, col ^ 1) for col in range(n_col)]
    chip_ring = [(col, (col + CORES) % n_col) for col in range(n_col)]

    def outward(value):
        return lax.ppermute(value, ("row", "col"), out_ring)

    def homeward(value):
        return lax.ppermute(value, ("row", "col"), back_ring)

    def to_sibling(value):
        return lax.ppermute(value, "col", sibling)

    def over_chips(value):
        parts = [value]
        for _ in range(n_x - 1):
            parts.append(lax.ppermute(parts[-1], "col", chip_ring))
        return parts

    def local(tokens, w_in, w_out, cotangent):
        rows, width = tokens.shape
        half = rows // 2
        units = w_in.shape[1]
        chain = Chain(None)
        order = list(range(far, -1, -1))

        def height(step):
            return rows if 0 < step < far else half

        share = sum(height(step) for step in order)

        def product(step, side):
            def body(ins, outs):
                left = [ins[0][half_at(0, half) if step == 0 else slice(None), pl.ds(band * width, width)]
                        for band in range(2)]
                for piece in tiles(units, 512):
                    part = jnp.dot(left[0], ins[1][:, piece], preferred_element_type=F32)
                    part = part + jnp.dot(left[1], ins[2][:, piece], preferred_element_type=F32)
                    outs[0][:, piece] = part.astype(BF16)

            weights = (w_out_t, w_out_t_far) if side else (w_in, w_in_far)
            total, = chain.run("product", body, [shape(height(step), units)], [blocks[step][side], *weights])
            sums[side, step] = over_chips(total)

        def own_other():
            def body(ins, outs):
                left = ins[0][half_at(1, half), :]
                for piece in tiles(units, 512):
                    outs[0][:, piece] = jnp.dot(left, ins[1][:, piece], preferred_element_type=F32).astype(BF16)

            return to_sibling(chain.run("own_other", body, [shape(half, units)], [tokens, w_in])[0])

        def own_mine(came):
            def body(ins, outs):
                left = ins[0][half_at(0, half), :]
                for piece in tiles(units, 512):
                    part = jnp.dot(left, ins[1][:, piece], preferred_element_type=F32)
                    outs[0][:, piece] = (part + ins[2][:, piece].astype(F32)).astype(BF16)

            total, = chain.run("own_mine", body, [shape(half, units)], [tokens, w_in, came])
            sums[0, 0] = over_chips(total)

        def both_bands(came):
            def body(ins, outs):
                for side in range(2):
                    outs[side][:, 0:width] = ins[side][...]
                    outs[side][:, width:2 * width] = ins[2 + side][...]

            return chain.run("both_bands", body, [shape(rows, 2 * width)] * 2, [tokens, cotangent, *came])

        def held(weights):
            def body(ins, outs):
                for ref, out in zip(ins, outs):
                    for piece in tiles(ref.shape[0], 256):
                        out[piece, :] = ref[piece, :]

            return chain.run("held", body, [shape(*weight.shape) for weight in weights], weights, False)

        def relay(step, side):
            def body(ins, outs):
                outs[0][...] = ins[0][...] if step + 1 < far else ins[0][half_at(0, half), :]

            size = shape(height(step + 1), 2 * width)
            blocks[step + 1][side] = outward(chain.run("relay", body, [size], [blocks[step][side]])[0])

        def gelu_of(value):
            cdf = 0.5 * (1.0 + lax.erf(value * 0.7071067811865476))
            pdf = jnp.exp(-0.5 * value * value) * 0.3989422804014327
            return value * cdf, cdf + value * pdf

        def gelu(step, also=()):
            def body(ins, outs):
                for strip in tiles(height(step), 16):
                    act_rows, slope_rows = gelu_of(added(ins, strip))
                    outs[0][strip, :] = act_rows.astype(BF16)
                    outs[1][strip, :] = slope_rows.astype(BF16)

            act[step], slope[step] = chain.run(
                "gelu", body, [shape(height(step), units)] * 2, sums[0, step], True, also)
            act_far[step] = to_sibling(act[step])

        def slopes(step, also=()):
            def body(ins, outs):
                for strip in tiles(height(step), 16):
                    value = added(ins[1:], strip) * ins[0][strip, :].astype(F32)
                    outs[0][strip, :] = value.astype(BF16)

            dpre[step], = chain.run(
                "slopes", body, [shape(height(step), units)], [slope[step]] + sums[1, step], True, also)
            dpre_far[step] = to_sibling(dpre[step])

        def term(step, hidden, weights, came=None):
            def body(ins, outs):
                for band in range(2):
                    for piece in tiles(width, 512):
                        part = jnp.dot(ins[0][...], ins[1 + band][:, piece], preferred_element_type=F32)
                        there = pl.ds(band * width + piece.start, piece.size)
                        if came is None:
                            outs[0][:, there] = part.astype(BF16)
                        elif step + 1 < far:
                            outs[0][:, there] = (part + ins[3][:, there].astype(F32)).astype(BF16)
                        else:
                            mine = half_at(0, half)
                            outs[0][:, there] = part.astype(BF16)
                            outs[0][mine, there] = (
                                outs[0][mine, there].astype(F32) + ins[3][:, there].astype(F32)).astype(BF16)

            ins = [hidden[step], *weights] + ([] if came is None else [came])
            return chain.run("term", body, [shape(height(step), 2 * width)], ins)[0]

        def joined(step, part, came):
            def body(ins, outs):
                if step + 1 < far:
                    for strip in tiles(rows, 16):
                        outs[0][strip, :] = added(ins, strip).astype(BF16)
                else:
                    outs[0][...] = ins[0][...]
                    mine = half_at(0, half)
                    outs[0][mine, :] = (ins[0][mine, :].astype(F32) + ins[1][...].astype(F32)).astype(BF16)

            return chain.run("joined", body, [shape(rows, 2 * width)], [part, came])[0]

        def settled(part, came):
            def body(ins, outs):
                mine = half_at(0, half)
                for band in range(2):
                    there = pl.ds(band * width, width)
                    outs[band][...] = ins[1][:, there]
                    outs[band][mine, :] = (
                        ins[1][mine, there].astype(F32) + ins[0][:, there].astype(F32)).astype(BF16)

            keep, give = chain.run("settled", body, [shape(rows, width)] * 2, [part, came])
            return keep, to_sibling(give)

        def finish(residual, keep, came):
            def body(ins, outs):
                outs[0][...] = added(ins, slice(None)).astype(BF16)

            return chain.run("finish", body, [shape(rows, width)], [residual, keep, came], False)[0]

        piece = rows // n_col

        def halved(part, came):
            def body(ins, outs):
                core = lax.axis_index("col") % CORES
                low = ins[0][...].astype(F32)
                zero = jnp.zeros_like(low)
                total = ins[1][...].astype(F32) + jnp.concatenate(
                    [jnp.where(core == 0, low, zero), jnp.where(core == 0, zero, low)])
                total = total.astype(BF16)
                for chip in range(n_x):
                    first, second = (
                        total[(2 * chip + index) * piece:(2 * chip + index + 1) * piece] for index in range(2))
                    outs[0][chip * piece:(chip + 1) * piece, :] = jnp.where(core == 0, first, second)
                    given = jnp.where(core == 0, second, first)
                    outs[1][chip * piece:(chip + 1) * piece, 0:width] = given[:, width:2 * width]
                    outs[1][chip * piece:(chip + 1) * piece, width:2 * width] = given[:, 0:width]

            keep, give = chain.run("halved", body, [shape(half, 2 * width)] * 2, [part, came])
            return keep, to_sibling(give)

        def spread(keep, other):
            def summed(ins, outs):
                col = lax.axis_index("col")
                core, here = col % CORES, col // CORES
                for offset in range(n_x):
                    chip = (here + offset) % n_x
                    there = pl.ds(pl.multiple_of(chip * piece, piece), piece)
                    stream = pl.ds(pl.multiple_of((chip * CORES + core) * piece, piece), piece)
                    outs[offset][...] = added(
                        [ins[0].at[there], ins[1].at[there], ins[2].at[stream]], slice(None)).astype(BF16)

            sent = chain.run(
                "summed", summed, [shape(piece, 2 * width)] * n_x, [keep, other, blocks[0][0]])
            bands = [sent[0]]
            for offset in range(1, n_x):
                pairs = [(col, (col + CORES * offset) % n_col) for col in range(n_col)]
                bands.append(lax.ppermute(sent[offset], "col", pairs))

            return bands

        def laid(bands):
            def body(ins, outs):
                col = lax.axis_index("col")
                core, here = col % CORES, col // CORES
                for offset in range(n_x):
                    chip = (here - offset + n_x) % n_x
                    for band in range(CORES):
                        start = (chip * CORES + (core + band) % CORES) * width
                        outs[0][:, pl.ds(pl.multiple_of(start, width), width)] = ins[offset][
                            :, band * width:(band + 1) * width]

            return chain.run("laid", body, [shape(piece, n_col * width)], bands)[0]

        def turned(weight):
            def body(ins, outs):
                for piece in tiles(weight.shape[0], 256):
                    outs[0][:, piece] = ins[0][piece, :].T

            return chain.run("turned", body, [shape(weight.shape[1], weight.shape[0])], [weight])[0]

        def packed_hidden(hidden, steps):
            def body(ins, outs):
                start = 0
                for ref, step in zip(ins, steps):
                    outs[0][start:start + height(step), :] = ref[...]
                    start += height(step)

            total = sum(height(step) for step in steps)
            return chain.run("packed", body, [shape(total, units)], [hidden[step] for step in steps], False)[0]

        def packed_stream():
            def body(ins, outs):
                for side in range(2):
                    start = 0
                    for ref, step in zip(ins[side::2], order):
                        size = height(step)
                        source = half_at(0, half) if step == 0 else pl.ds(0, size)
                        outs[side][start:start + size, :] = ref[source, 0:width]
                        outs[2][side * share + start:side * share + start + size, :] = ref[source, width:2 * width]
                        start += size

            outs = [shape(share, width)] * 2 + [shape(2 * share, width)]
            tok, cot, give = chain.run("packed", body, outs, [block for step in order for block in blocks[step]], False)
            return tok, cot, to_sibling(give)

        sums, act, slope, dpre, act_term, act_far, dpre_far = {}, {}, {}, {}, {}, {}, {}
        blocks = {step: [None, None] for step in range(far + 1)}
        everything = slice(None)

        stream = [to_sibling(tokens), to_sibling(cotangent)]
        came = own_other()
        blocks[0] = both_bands(stream)
        blocks[1] = [outward(block) for block in blocks[0]]
        own_mine(came)
        w_in_far, w_out_far = (to_sibling(weight) for weight in held([w_in, w_out]))

        for step in range(1, far + 1):
            if step < far:
                relay(step, 0)
            product(step, 0)
            if step < far:
                gelu(step - 1, [act_far[step - 2]] if step > 1 else [])
                relay(step, 1)
            if step == 1:
                w_in_t, w_in_t_far = turned(w_in), turned(w_in_far)
            if step == 2:
                w_out_t, w_out_t_far = turned(w_out), turned(w_out_far)
            elif 2 < step < far:
                act_term[step - 3] = term(step - 3, act, (w_out, w_out_far))
        product(far, 1)
        act_term[max(far - 3, 0)] = term(max(far - 3, 0), act, (w_out, w_out_far))
        gelu(far - 1, [act_far[far - 2]])
        tok_own, cot_own, stream_far = packed_stream()
        for step in range(max(far - 3, 0) + 1, far):
            act_term[step] = term(step, act, (w_out, w_out_far))
        product(far - 1, 1)
        gelu(far, [act_far[far - 1], stream_far])
        going = homeward(term(far, act, (w_out, w_out_far)))
        back_going = grad_out = None
        for step in range(far, 1, -1):
            slopes(step, [act_far[far] if step == far else dpre_far[step + 1]])
            back_going = homeward(term(step, dpre, (w_in_t, w_in_t_far), back_going))
            going = homeward(joined(step - 1, act_term[step - 1], going))
            product(step - 2, 1)
            if far - 1 <= step:
                grad_out = chain.outer("grad_out", [
                    (packed_hidden(act, order), everything, cot_own, everything),
                    (packed_hidden(act_far, order), everything, stream_far, pl.ds(share, share)),
                ], grad_out, (far - step, 2))
        slopes(1, [dpre_far[2]])
        back_going = homeward(term(1, dpre, (w_in_t, w_in_t_far), back_going))
        row_shares = halved(act_term[0], going)
        slopes(0)
        back_own = term(0, dpre, (w_in_t, w_in_t_far))
        bands = spread(*row_shares)
        grad_in = chain.outer("grad_in", [
            (tok_own, everything, packed_hidden(dpre, order), everything),
            (stream_far, pl.ds(0, share), packed_hidden(dpre_far, order), everything),
        ])
        block_out = laid(bands)
        grad_tokens = finish(cotangent, *settled(back_own, back_going))
        return block_out, grad_tokens, grad_in, grad_out

    in_specs = (P("row", "col"), P("col", "row"), P("row", "col"), P("row", "col"))
    out_specs = (P(("row", "col"), None), P("row", "col"), P("col", "row"), P("row", "col"))
    return jax.shard_map(local, mesh=mesh, in_specs=in_specs, out_specs=out_specs, check_vma=False)
```

```python
import jax
import jax.numpy as jnp
from jax import lax
from jax.experimental import pallas as pl
from jax.experimental.pallas import tpu as pltpu
from jax.sharding import PartitionSpec as P

CORES = 2
ROOM = 61
F32 = jnp.float32
BF16 = jnp.bfloat16
MIB = 2 ** 20
IN_VMEM = pl.BlockSpec(memory_space=pltpu.VMEM)
IN_HBM = pl.BlockSpec(memory_space=pltpu.HBM)
ANYWHERE = pl.BlockSpec(memory_space=pl.ANY)
MICROSECOND = 10 ** 9
COSTS = {"grad_out": 6.0, "grad_in": 0.1, "laid": 0.1, "grad_in_early": 6.0, "grad_out_early": 6.0, "summed": 0.3, "settled": 0.3}
USUAL_COST = 3.0


def cost(name):
    return pl.CostEstimate(
        flops=int(COSTS.get(name, USUAL_COST) * MICROSECOND), bytes_accessed=0, transcendentals=0)


def ring_order(count):
    if count % 4:
        return list(range(count))
    minor = count // 4
    order = [major * minor for major in range(4)]
    for turn, major in enumerate(reversed(range(4))):
        steps = range(1, minor) if turn % 2 == 0 else range(minor - 1, 0, -1)
        order += [major * minor + step for step in steps]
    return order


def ring_pairs(count, n_col, sign):
    order = ring_order(count)
    pairs = []
    for place in range(count):
        for col in range(n_col):
            step = sign if col % CORES == 0 else -sign
            target = order[(place + step) % count]
            pairs.append((order[place] * n_col + col, target * n_col + col))
    return pairs


def shape(rows, columns):
    return jax.ShapeDtypeStruct((rows, columns), BF16)


def half_at(which, half, base=0):
    core = lax.axis_index("col") % CORES
    return pl.ds(pl.multiple_of((core if which == 0 else 1 - core) * half + base, half), half)


def tiles(extent, size):
    return [pl.ds(start, min(size, extent - start)) for start in range(0, extent, size)]


def added(refs, strip):
    total = refs[0][strip, :].astype(F32)
    for ref in refs[1:]:
        total = total + ref[strip, :].astype(F32)
    return total


class Chain:
    def __init__(self, first):
        self.last = first

    def run(self, name, body, outs, ins, holds=True, also=(), in_spec=IN_VMEM, scratch=(), room=6):
        behind = [*([] if self.last is None else [self.last]), *also]

        def kernel(*refs):
            body(refs[len(behind):len(behind) + len(ins)], refs[len(behind) + len(ins):])

        result = pl.pallas_call(
            kernel,
            out_shape=outs,
            in_specs=[ANYWHERE] * len(behind) + [in_spec] * len(ins),
            out_specs=[IN_VMEM] * len(outs),
            scratch_shapes=list(scratch),
            compiler_params=pltpu.CompilerParams(vmem_limit_bytes=room * MIB),
            cost_estimate=cost(name),
            name=name,
        )(*behind, *ins)
        if holds:
            self.last = result[0]
        return result

    def outer(self, name, pairs, begun=None, part=(0, 1)):
        arrays = [array for left, _, right, _ in pairs for array in (left, right)]
        out = jax.ShapeDtypeStruct((pairs[0][0].shape[1], pairs[0][2].shape[1]), F32)
        tile = min(512, out.shape[0] // part[1])
        steps = out.shape[0] // tile // part[1]
        first = part[0] * steps
        bands = pl.BlockSpec((tile, out.shape[1]), lambda band: (band + first, 0))
        more = [] if begun is None else [begun]

        def kernel(after_ref, *refs):
            band = pl.ds(pl.multiple_of((pl.program_id(0) + first) * tile, tile), tile)
            total = None
            for index, (_, left_rows, _, right_rows) in enumerate(pairs):
                product = lax.dot_general(
                    refs[2 * index][left_rows, band], refs[2 * index + 1][right_rows, :],
                    (((0,), (0,)), ((), ())), preferred_element_type=F32)
                total = product if total is None else total + product
            refs[-2][...] = total
            refs[-1][...] = jnp.zeros_like(refs[-1])

        result, self.last = pl.pallas_call(
            kernel,
            grid=(steps,),
            out_shape=[out, shape(16, 128)],
            in_specs=[ANYWHERE] + [IN_VMEM] * len(arrays) + [ANYWHERE] * len(more),
            out_specs=[bands, IN_VMEM],
            input_output_aliases={1 + len(arrays): 0} if more else {},
            compiler_params=pltpu.CompilerParams(vmem_limit_bytes=(14 if out.shape[1] <= 1024 else 24) * MIB),
            cost_estimate=cost(name),
            name=name,
        )(self.last, *arrays, *more)
        return result


def solution(mesh):
    n_row, n_col = mesh.shape["row"], mesh.shape["col"]
    n_x = n_col // CORES
    far = n_row // 2
    out_ring = ring_pairs(n_row, n_col, 1)
    back_ring = ring_pairs(n_row, n_col, -1)
    sibling = [(col, col ^ 1) for col in range(n_col)]
    chip_ring = [(col, (col + CORES) % n_col) for col in range(n_col)]

    def outward(value):
        return lax.ppermute(value, ("row", "col"), out_ring)

    def homeward(value):
        return lax.ppermute(value, ("row", "col"), back_ring)

    def to_sibling(value):
        return lax.ppermute(value, "col", sibling)

    def over_chips(value):
        parts = [value]
        for _ in range(n_x - 1):
            parts.append(lax.ppermute(parts[-1], "col", chip_ring))
        return parts

    def local(tokens, w_in, w_out, cotangent):
        rows, width = tokens.shape
        half = rows // 2
        units = w_in.shape[1]
        chain = Chain(None)
        order = list(range(far, -1, -1))

        def height(step):
            return rows if 0 < step < far else half

        share = sum(height(step) for step in order)

        def product(step, side):
            def body(ins, outs):
                left = [ins[0][half_at(0, half) if step == 0 else slice(None), pl.ds(band * width, width)]
                        for band in range(2)]
                for piece in tiles(units, 512):
                    part = jnp.dot(left[0], ins[1][:, piece], preferred_element_type=F32)
                    part = part + jnp.dot(left[1], ins[2][:, piece], preferred_element_type=F32)
                    outs[0][:, piece] = part.astype(BF16)

            weights = (w_out_t, w_out_t_far) if side else (w_in, w_in_far)
            total, = chain.run("product", body, [shape(height(step), units)], [blocks[step][side], *weights])
            sums[side, step] = over_chips(total)

        def own_other():
            cuts = tiles(width, max(width // 4, 128))

            def body(ins, outs):
                product, left_ref, weight_ref, done = outs
                copies = [pltpu.make_async_copy(ins[0].at[half_at(1, half)], left_ref, done.at[len(cuts)])]
                for index, piece in enumerate(cuts):
                    copies.append(pltpu.make_async_copy(
                        ins[1].at[piece], weight_ref.at[piece], done.at[index]))
                for copy in copies:
                    copy.start()
                copies[0].wait()
                total = jnp.zeros((half, units), F32)
                for copy, piece in zip(copies[1:], cuts):
                    copy.wait()
                    total = total + jnp.dot(
                        left_ref[:, piece], weight_ref[piece, :], preferred_element_type=F32)
                product[...] = total.astype(BF16)

            scratch = [pltpu.VMEM((half, width), BF16), pltpu.VMEM(w_in.shape, BF16),
                       pltpu.SemaphoreType.DMA((len(cuts) + 1,))]
            return to_sibling(chain.run(
                "own_other", body, [shape(half, units)], [tokens, w_in],
                in_spec=IN_HBM, scratch=scratch, room=ROOM)[0])

        def own_mine(came):
            def body(ins, outs):
                left = ins[0][half_at(0, half), :]
                for piece in tiles(units, 512):
                    part = jnp.dot(left, ins[1][:, piece], preferred_element_type=F32)
                    outs[0][:, piece] = (part + ins[2][:, piece].astype(F32)).astype(BF16)

            total, = chain.run("own_mine", body, [shape(half, units)], [tokens, w_in, came])
            sums[0, 0] = over_chips(total)

        def both_bands(came):
            def body(ins, outs):
                for side in range(2):
                    outs[side][:, 0:width] = ins[side][...]
                    outs[side][:, width:2 * width] = ins[2 + side][...]

            return chain.run("both_bands", body, [shape(rows, 2 * width)] * 2, [tokens, cotangent, *came])

        def held(weights):
            def body(ins, outs):
                for ref, out in zip(ins, outs):
                    for piece in tiles(ref.shape[0], 256):
                        out[piece, :] = ref[piece, :]

            return chain.run("held", body, [shape(*weight.shape) for weight in weights], weights, False)

        def relay(step, side):
            def body(ins, outs):
                outs[0][...] = ins[0][...] if step + 1 < far else ins[0][half_at(0, half), :]

            size = shape(height(step + 1), 2 * width)
            blocks[step + 1][side] = outward(chain.run("relay", body, [size], [blocks[step][side]])[0])

        def gelu_of(value):
            cdf = 0.5 * (1.0 + lax.erf(value * 0.7071067811865476))
            pdf = jnp.exp(-0.5 * value * value) * 0.3989422804014327
            return value * cdf, cdf + value * pdf

        def gelu(step, also=()):
            def body(ins, outs):
                for strip in tiles(height(step), 16):
                    act_rows, slope_rows = gelu_of(added(ins, strip))
                    outs[0][strip, :] = act_rows.astype(BF16)
                    outs[1][strip, :] = slope_rows.astype(BF16)

            act[step], slope[step] = chain.run(
                "gelu", body, [shape(height(step), units)] * 2, sums[0, step], True, also)
            act_far[step] = to_sibling(act[step])

        def slopes(step, also=()):
            def body(ins, outs):
                for strip in tiles(height(step), 16):
                    value = added(ins[1:], strip) * ins[0][strip, :].astype(F32)
                    outs[0][strip, :] = value.astype(BF16)

            dpre[step], = chain.run(
                "slopes", body, [shape(height(step), units)], [slope[step]] + sums[1, step], True, also)
            dpre_far[step] = to_sibling(dpre[step])

        def term(step, hidden, weights, came=None):
            def body(ins, outs):
                for band in range(2):
                    for piece in tiles(width, 512):
                        part = jnp.dot(ins[0][...], ins[1 + band][:, piece], preferred_element_type=F32)
                        there = pl.ds(band * width + piece.start, piece.size)
                        if came is None:
                            outs[0][:, there] = part.astype(BF16)
                        elif step + 1 < far:
                            outs[0][:, there] = (part + ins[3][:, there].astype(F32)).astype(BF16)
                        else:
                            mine = half_at(0, half)
                            outs[0][:, there] = part.astype(BF16)
                            outs[0][mine, there] = (
                                outs[0][mine, there].astype(F32) + ins[3][:, there].astype(F32)).astype(BF16)

            ins = [hidden[step], *weights] + ([] if came is None else [came])
            return chain.run("term", body, [shape(height(step), 2 * width)], ins)[0]

        def joined(step, part, came):
            def body(ins, outs):
                if step + 1 < far:
                    for strip in tiles(rows, 16):
                        outs[0][strip, :] = added(ins, strip).astype(BF16)
                else:
                    outs[0][...] = ins[0][...]
                    mine = half_at(0, half)
                    outs[0][mine, :] = (ins[0][mine, :].astype(F32) + ins[1][...].astype(F32)).astype(BF16)

            return chain.run("joined", body, [shape(rows, 2 * width)], [part, came])[0]

        def settled(part, came):
            def body(ins, outs):
                mine = half_at(0, half)
                for band in range(2):
                    there = pl.ds(band * width, width)
                    outs[band][...] = ins[1][:, there]
                    outs[band][mine, :] = (
                        ins[1][mine, there].astype(F32) + ins[0][:, there].astype(F32)).astype(BF16)

            keep, give = chain.run("settled", body, [shape(rows, width)] * 2, [part, came])
            return keep, to_sibling(give)

        piece = rows // n_col

        def halved(part, came):
            def body(ins, outs):
                core = lax.axis_index("col") % CORES
                low = ins[0][...].astype(F32)
                zero = jnp.zeros_like(low)
                total = ins[1][...].astype(F32) + jnp.concatenate(
                    [jnp.where(core == 0, low, zero), jnp.where(core == 0, zero, low)])
                total = total.astype(BF16)
                for chip in range(n_x):
                    first, second = (
                        total[(2 * chip + index) * piece:(2 * chip + index + 1) * piece] for index in range(2))
                    outs[0][chip * piece:(chip + 1) * piece, :] = jnp.where(core == 0, first, second)
                    given = jnp.where(core == 0, second, first)
                    outs[1][chip * piece:(chip + 1) * piece, 0:width] = given[:, width:2 * width]
                    outs[1][chip * piece:(chip + 1) * piece, width:2 * width] = given[:, 0:width]

            keep, give = chain.run("halved", body, [shape(half, 2 * width)] * 2, [part, came])
            return keep, to_sibling(give)

        def spread(keep, other):
            def summed(ins, outs):
                col = lax.axis_index("col")
                core, here = col % CORES, col // CORES
                for offset in range(n_x):
                    chip = (here + offset) % n_x
                    there = pl.ds(pl.multiple_of(chip * piece, piece), piece)
                    stream = pl.ds(pl.multiple_of((chip * CORES + core) * piece, piece), piece)
                    outs[offset][...] = added(
                        [ins[0].at[there], ins[1].at[there], ins[2].at[stream]], slice(None)).astype(BF16)

            sent = chain.run(
                "summed", summed, [shape(piece, 2 * width)] * n_x, [keep, other, blocks[0][0]])
            bands = [sent[0]]
            for offset in range(1, n_x):
                pairs = [(col, (col + CORES * offset) % n_col) for col in range(n_col)]
                bands.append(lax.ppermute(sent[offset], "col", pairs))

            return bands

        def finish(bands, terms):
            def body(ins, outs):
                col = lax.axis_index("col")
                core, here = col % CORES, col // CORES
                for offset in range(n_x):
                    chip = (here - offset + n_x) % n_x
                    for band in range(CORES):
                        start = (chip * CORES + (core + band) % CORES) * width
                        outs[0][:, pl.ds(pl.multiple_of(start, width), width)] = ins[offset][
                            :, band * width:(band + 1) * width]
                outs[1][...] = added(ins[n_x:], slice(None)).astype(BF16)

            return chain.run("finish", body, [shape(piece, n_col * width), shape(rows, width)], [*bands, *terms])

        def turned(weight):
            def body(ins, outs):
                for piece in tiles(weight.shape[0], 256):
                    outs[0][:, piece] = ins[0][piece, :].T

            return chain.run("turned", body, [shape(weight.shape[1], weight.shape[0])], [weight])[0]

        def packed_hidden(hidden, steps):
            def body(ins, outs):
                start = 0
                for ref, step in zip(ins, steps):
                    outs[0][start:start + height(step), :] = ref[...]
                    start += height(step)

            total = sum(height(step) for step in steps)
            return chain.run("packed", body, [shape(total, units)], [hidden[step] for step in steps], False)[0]

        def packed_stream():
            def body(ins, outs):
                for side in range(2):
                    start = 0
                    for ref, step in zip(ins[side::2], order):
                        size = height(step)
                        source = half_at(0, half) if step == 0 else pl.ds(0, size)
                        outs[side][start:start + size, :] = ref[source, 0:width]
                        outs[2][side * share + start:side * share + start + size, :] = ref[source, width:2 * width]
                        start += size

            outs = [shape(share, width)] * 2 + [shape(2 * share, width)]
            tok, cot, give = chain.run("packed", body, outs, [block for step in order for block in blocks[step]], False)
            return tok, cot, to_sibling(give)

        sums, act, slope, dpre, act_term, act_far, dpre_far = {}, {}, {}, {}, {}, {}, {}
        blocks = {step: [None, None] for step in range(far + 1)}
        everything = slice(None)

        stream = [to_sibling(tokens), to_sibling(cotangent)]
        came = own_other()
        blocks[0] = both_bands(stream)
        blocks[1] = [outward(block) for block in blocks[0]]
        own_mine(came)
        w_in_far, w_out_far = (to_sibling(weight) for weight in held([w_in, w_out]))

        for step in range(1, far + 1):
            if step < far:
                relay(step, 0)
            product(step, 0)
            if step < far:
                gelu(step - 1, [act_far[step - 2]] if step > 1 else [])
                relay(step, 1)
            if step == 1:
                w_in_t, w_in_t_far = turned(w_in), turned(w_in_far)
            if step == 2:
                w_out_t, w_out_t_far = turned(w_out), turned(w_out_far)
            elif 2 < step < far:
                act_term[step - 3] = term(step - 3, act, (w_out, w_out_far))
        product(far, 1)
        act_term[max(far - 3, 0)] = term(max(far - 3, 0), act, (w_out, w_out_far))
        gelu(far - 1, [act_far[far - 2]])
        tok_own, cot_own, stream_far = packed_stream()
        for step in range(max(far - 3, 0) + 1, far):
            act_term[step] = term(step, act, (w_out, w_out_far))
        product(far - 1, 1)
        gelu(far, [act_far[far - 1], stream_far])
        going = homeward(term(far, act, (w_out, w_out_far)))
        back_going = grad_out = None
        for step in range(far, 1, -1):
            slopes(step, [act_far[far] if step == far else dpre_far[step + 1]])
            back_going = homeward(term(step, dpre, (w_in_t, w_in_t_far), back_going))
            going = homeward(joined(step - 1, act_term[step - 1], going))
            product(step - 2, 1)
            if far - 1 <= step:
                grad_out = chain.outer("grad_out", [
                    (packed_hidden(act, order), everything, cot_own, everything),
                    (packed_hidden(act_far, order), everything, stream_far, pl.ds(share, share)),
                ], grad_out, (far - step, 2))
        slopes(1, [dpre_far[2]])
        back_going = homeward(term(1, dpre, (w_in_t, w_in_t_far), back_going))
        row_shares = halved(act_term[0], going)
        slopes(0)
        back_own = term(0, dpre, (w_in_t, w_in_t_far))
        bands = spread(*row_shares)
        dpre_own, dpre_other = packed_hidden(dpre, order), packed_hidden(dpre_far, order)
        grad_in = None
        for index in range(2):
            grad_in = chain.outer("grad_in", [
                (tok_own, everything, dpre_own, everything),
                (stream_far, pl.ds(0, share), dpre_other, everything),
            ], grad_in, (index, 2))
            if index == 0:
                keep, came = settled(back_own, back_going)
        block_out, grad_tokens = finish(bands, [cotangent, keep, came])
        return block_out, grad_tokens, grad_in, grad_out

    in_specs = (P("row", "col"), P("col", "row"), P("row", "col"), P("row", "col"))
    out_specs = (P(("row", "col"), None), P("row", "col"), P("col", "row"), P("row", "col"))
    return jax.shard_map(local, mesh=mesh, in_specs=in_specs, out_specs=out_specs, check_vma=False)
```

```python
import jax
import jax.numpy as jnp
from jax import lax
from jax.experimental import pallas as pl
from jax.experimental.pallas import tpu as pltpu
from jax.sharding import PartitionSpec as P

CORES = 2
ROOM = 61
F32 = jnp.float32
BF16 = jnp.bfloat16
MIB = 2 ** 20
IN_VMEM = pl.BlockSpec(memory_space=pltpu.VMEM)
IN_HBM = pl.BlockSpec(memory_space=pltpu.HBM)
ANYWHERE = pl.BlockSpec(memory_space=pl.ANY)
MICROSECOND = 10 ** 9
COSTS = {"grad_out": 6.0, "grad_in": 0.1, "laid": 0.1, "grad_in_early": 6.0, "grad_out_early": 6.0, "summed": 0.3, "settled": 0.3, "arrived": 0.1}
USUAL_COST = 3.0


def cost(name):
    return pl.CostEstimate(
        flops=int(COSTS.get(name, USUAL_COST) * MICROSECOND), bytes_accessed=0, transcendentals=0)


def ring_order(count):
    if count % 4:
        return list(range(count))
    minor = count // 4
    order = [major * minor for major in range(4)]
    for turn, major in enumerate(reversed(range(4))):
        steps = range(1, minor) if turn % 2 == 0 else range(minor - 1, 0, -1)
        order += [major * minor + step for step in steps]
    return order


def ring_pairs(count, n_col, sign):
    order = ring_order(count)
    pairs = []
    for place in range(count):
        for col in range(n_col):
            step = sign if col % CORES == 0 else -sign
            target = order[(place + step) % count]
            pairs.append((order[place] * n_col + col, target * n_col + col))
    return pairs


def shape(rows, columns):
    return jax.ShapeDtypeStruct((rows, columns), BF16)


def half_at(which, half, base=0):
    core = lax.axis_index("col") % CORES
    return pl.ds(pl.multiple_of((core if which == 0 else 1 - core) * half + base, half), half)


def tiles(extent, size):
    return [pl.ds(start, min(size, extent - start)) for start in range(0, extent, size)]


def added(refs, strip):
    total = refs[0][strip, :].astype(F32)
    for ref in refs[1:]:
        total = total + ref[strip, :].astype(F32)
    return total


class Chain:
    def __init__(self, first):
        self.last = first

    def run(self, name, body, outs, ins, holds=True, also=(), in_spec=IN_VMEM, scratch=(), room=6):
        behind = [*([] if self.last is None else [self.last]), *also]

        def kernel(*refs):
            body(refs[len(behind):len(behind) + len(ins)], refs[len(behind) + len(ins):])

        result = pl.pallas_call(
            kernel,
            out_shape=outs,
            in_specs=[ANYWHERE] * len(behind) + [in_spec] * len(ins),
            out_specs=[IN_VMEM] * len(outs),
            scratch_shapes=list(scratch),
            compiler_params=pltpu.CompilerParams(vmem_limit_bytes=room * MIB),
            cost_estimate=cost(name),
            name=name,
        )(*behind, *ins)
        if holds:
            self.last = result[0]
        return result

    def outer(self, name, pairs, begun=None, part=(0, 1)):
        arrays = [array for left, _, right, _ in pairs for array in (left, right)]
        out = jax.ShapeDtypeStruct((pairs[0][0].shape[1], pairs[0][2].shape[1]), F32)
        tile = min(512, out.shape[0] // part[1])
        steps = out.shape[0] // tile // part[1]
        first = part[0] * steps
        bands = pl.BlockSpec((tile, out.shape[1]), lambda band: (band + first, 0))
        more = [] if begun is None else [begun]

        def kernel(after_ref, *refs):
            band = pl.ds(pl.multiple_of((pl.program_id(0) + first) * tile, tile), tile)
            total = None
            for index, (_, left_rows, _, right_rows) in enumerate(pairs):
                product = lax.dot_general(
                    refs[2 * index][left_rows, band], refs[2 * index + 1][right_rows, :],
                    (((0,), (0,)), ((), ())), preferred_element_type=F32)
                total = product if total is None else total + product
            refs[-2][...] = total
            refs[-1][...] = jnp.zeros_like(refs[-1])

        result, self.last = pl.pallas_call(
            kernel,
            grid=(steps,),
            out_shape=[out, shape(16, 128)],
            in_specs=[ANYWHERE] + [IN_VMEM] * len(arrays) + [ANYWHERE] * len(more),
            out_specs=[bands, IN_VMEM],
            input_output_aliases={1 + len(arrays): 0} if more else {},
            compiler_params=pltpu.CompilerParams(vmem_limit_bytes=(14 if out.shape[1] <= 1024 else 24) * MIB),
            cost_estimate=cost(name),
            name=name,
        )(self.last, *arrays, *more)
        return result


def solution(mesh):
    n_row, n_col = mesh.shape["row"], mesh.shape["col"]
    n_x = n_col // CORES
    far = n_row // 2
    out_ring = ring_pairs(n_row, n_col, 1)
    back_ring = ring_pairs(n_row, n_col, -1)
    sibling = [(col, col ^ 1) for col in range(n_col)]
    chip_ring = [(col, (col + CORES) % n_col) for col in range(n_col)]

    def outward(value):
        return lax.ppermute(value, ("row", "col"), out_ring)

    def homeward(value):
        return lax.ppermute(value, ("row", "col"), back_ring)

    def to_sibling(value):
        return lax.ppermute(value, "col", sibling)

    def over_chips(value):
        parts = [value]
        for _ in range(n_x - 1):
            parts.append(lax.ppermute(parts[-1], "col", chip_ring))
        return parts

    def local(tokens, w_in, w_out, cotangent):
        rows, width = tokens.shape
        half = rows // 2
        units = w_in.shape[1]
        chain = Chain(None)
        order = list(range(far, -1, -1))

        def height(step):
            return rows if 0 < step < far else half

        share = sum(height(step) for step in order)

        def product(step, side):
            def body(ins, outs):
                left = [ins[0][half_at(0, half) if step == 0 else slice(None), pl.ds(band * width, width)]
                        for band in range(2)]
                for piece in tiles(units, 512):
                    part = jnp.dot(left[0], ins[1][:, piece], preferred_element_type=F32)
                    part = part + jnp.dot(left[1], ins[2][:, piece], preferred_element_type=F32)
                    outs[0][:, piece] = part.astype(BF16)

            weights = (w_out_t, w_out_t_far) if side else (w_in, w_in_far)
            total, = chain.run("product", body, [shape(height(step), units)], [blocks[step][side], *weights])
            sums[side, step] = over_chips(total)

        def own_other():
            cuts = tiles(width, max(width // 4, 128))

            def body(ins, outs):
                product, left_ref, weight_ref, done = outs
                copies = [pltpu.make_async_copy(ins[0].at[half_at(1, half)], left_ref, done.at[len(cuts)])]
                for index, piece in enumerate(cuts):
                    copies.append(pltpu.make_async_copy(
                        ins[1].at[piece], weight_ref.at[piece], done.at[index]))
                for copy in copies:
                    copy.start()
                copies[0].wait()
                total = jnp.zeros((half, units), F32)
                for copy, piece in zip(copies[1:], cuts):
                    copy.wait()
                    total = total + jnp.dot(
                        left_ref[:, piece], weight_ref[piece, :], preferred_element_type=F32)
                product[...] = total.astype(BF16)

            scratch = [pltpu.VMEM((half, width), BF16), pltpu.VMEM(w_in.shape, BF16),
                       pltpu.SemaphoreType.DMA((len(cuts) + 1,))]
            return to_sibling(chain.run(
                "own_other", body, [shape(half, units)], [tokens, w_in],
                in_spec=IN_HBM, scratch=scratch, room=ROOM)[0])

        def own_mine(came):
            def body(ins, outs):
                left = ins[0][half_at(0, half), :]
                for piece in tiles(units, 512):
                    part = jnp.dot(left, ins[1][:, piece], preferred_element_type=F32)
                    outs[0][:, piece] = (part + ins[2][:, piece].astype(F32)).astype(BF16)

            total, = chain.run("own_mine", body, [shape(half, units)], [tokens, w_in, came])
            sums[0, 0] = over_chips(total)

        def both_bands(came):
            def body(ins, outs):
                for side in range(2):
                    outs[side][:, 0:width] = ins[side][...]
                    outs[side][:, width:2 * width] = ins[2 + side][...]

            return chain.run("both_bands", body, [shape(rows, 2 * width)] * 2, [tokens, cotangent, *came])

        def held(weights):
            def body(ins, outs):
                for ref, out in zip(ins, outs):
                    for piece in tiles(ref.shape[0], 256):
                        out[piece, :] = ref[piece, :]

            return chain.run("held", body, [shape(*weight.shape) for weight in weights], weights, False)

        def relay(step, side):
            def body(ins, outs):
                outs[0][...] = ins[0][...] if step + 1 < far else ins[0][half_at(0, half), :]

            size = shape(height(step + 1), 2 * width)
            blocks[step + 1][side] = outward(chain.run("relay", body, [size], [blocks[step][side]])[0])

        def gelu_of(value):
            cdf = 0.5 * (1.0 + lax.erf(value * 0.7071067811865476))
            pdf = jnp.exp(-0.5 * value * value) * 0.3989422804014327
            return value * cdf, cdf + value * pdf

        def gelu(step, also=()):
            def body(ins, outs):
                for strip in tiles(height(step), 16):
                    act_rows, slope_rows = gelu_of(added(ins, strip))
                    outs[0][strip, :] = act_rows.astype(BF16)
                    outs[1][strip, :] = slope_rows.astype(BF16)

            act[step], slope[step] = chain.run(
                "gelu", body, [shape(height(step), units)] * 2, sums[0, step], True, also)
            act_far[step] = to_sibling(act[step])

        def slopes(step, also=()):
            def body(ins, outs):
                for strip in tiles(height(step), 16):
                    value = added(ins[1:], strip) * ins[0][strip, :].astype(F32)
                    outs[0][strip, :] = value.astype(BF16)

            dpre[step], = chain.run(
                "slopes", body, [shape(height(step), units)], [slope[step]] + sums[1, step], True, also)
            dpre_far[step] = to_sibling(dpre[step])

        def term(step, hidden, weights, came=None):
            def body(ins, outs):
                for band in range(2):
                    for piece in tiles(width, 512):
                        part = jnp.dot(ins[0][...], ins[1 + band][:, piece], preferred_element_type=F32)
                        there = pl.ds(band * width + piece.start, piece.size)
                        if came is None:
                            outs[0][:, there] = part.astype(BF16)
                        elif step + 1 < far:
                            outs[0][:, there] = (part + ins[3][:, there].astype(F32)).astype(BF16)
                        else:
                            mine = half_at(0, half)
                            outs[0][:, there] = part.astype(BF16)
                            outs[0][mine, there] = (
                                outs[0][mine, there].astype(F32) + ins[3][:, there].astype(F32)).astype(BF16)

            ins = [hidden[step], *weights] + ([] if came is None else [came])
            return chain.run("term", body, [shape(height(step), 2 * width)], ins)[0]

        def joined(step, part, came):
            def body(ins, outs):
                if step + 1 < far:
                    for strip in tiles(rows, 16):
                        outs[0][strip, :] = added(ins, strip).astype(BF16)
                else:
                    outs[0][...] = ins[0][...]
                    mine = half_at(0, half)
                    outs[0][mine, :] = (ins[0][mine, :].astype(F32) + ins[1][...].astype(F32)).astype(BF16)

            return chain.run("joined", body, [shape(rows, 2 * width)], [part, came])[0]

        def settled(part, came):
            def body(ins, outs):
                mine = half_at(0, half)
                for band in range(2):
                    there = pl.ds(band * width, width)
                    outs[band][...] = ins[1][:, there]
                    outs[band][mine, :] = (
                        ins[1][mine, there].astype(F32) + ins[0][:, there].astype(F32)).astype(BF16)

            keep, give = chain.run("settled", body, [shape(rows, width)] * 2, [part, came])
            return keep, to_sibling(give)

        piece = rows // n_col

        def halved(part, came):
            def body(ins, outs):
                core = lax.axis_index("col") % CORES
                low = ins[0][...].astype(F32)
                zero = jnp.zeros_like(low)
                total = ins[1][...].astype(F32) + jnp.concatenate(
                    [jnp.where(core == 0, low, zero), jnp.where(core == 0, zero, low)])
                total = total.astype(BF16)
                for chip in range(n_x):
                    first, second = (
                        total[(2 * chip + index) * piece:(2 * chip + index + 1) * piece] for index in range(2))
                    outs[0][chip * piece:(chip + 1) * piece, :] = jnp.where(core == 0, first, second)
                    given = jnp.where(core == 0, second, first)
                    outs[1][chip * piece:(chip + 1) * piece, 0:width] = given[:, width:2 * width]
                    outs[1][chip * piece:(chip + 1) * piece, width:2 * width] = given[:, 0:width]

            keep, give = chain.run("halved", body, [shape(half, 2 * width)] * 2, [part, came])
            return keep, to_sibling(give)

        def spread(keep, other):
            def summed(ins, outs):
                col = lax.axis_index("col")
                core, here = col % CORES, col // CORES
                for offset in range(n_x):
                    chip = (here + offset) % n_x
                    there = pl.ds(pl.multiple_of(chip * piece, piece), piece)
                    stream = pl.ds(pl.multiple_of((chip * CORES + core) * piece, piece), piece)
                    outs[offset][...] = added(
                        [ins[0].at[there], ins[1].at[there], ins[2].at[stream]], slice(None)).astype(BF16)

            sent = chain.run(
                "summed", summed, [shape(piece, 2 * width)] * n_x, [keep, other, blocks[0][0]])
            bands = [sent[0]]
            for offset in range(1, n_x):
                pairs = [(col, (col + CORES * offset) % n_col) for col in range(n_col)]
                bands.append(lax.ppermute(sent[offset], "col", pairs))

            return bands

        def finish(bands, terms):
            def body(ins, outs):
                col = lax.axis_index("col")
                core, here = col % CORES, col // CORES
                for offset in range(n_x):
                    chip = (here - offset + n_x) % n_x
                    for band in range(CORES):
                        start = (chip * CORES + (core + band) % CORES) * width
                        outs[0][:, pl.ds(pl.multiple_of(start, width), width)] = ins[offset][
                            :, band * width:(band + 1) * width]
                outs[1][...] = added(ins[n_x:], slice(None)).astype(BF16)

            return chain.run("finish", body, [shape(piece, n_col * width), shape(rows, width)], [*bands, *terms])

        def arrived(parts):
            def body(ins, outs):
                outs[0][...] = jnp.zeros_like(outs[0])

            chain.run("arrived", body, [shape(16, 128)], [], True, parts)

        def turned(weight):
            def body(ins, outs):
                for piece in tiles(weight.shape[0], 256):
                    outs[0][:, piece] = ins[0][piece, :].T

            return chain.run("turned", body, [shape(weight.shape[1], weight.shape[0])], [weight])[0]

        def packed_hidden(hidden, steps):
            def body(ins, outs):
                start = 0
                for ref, step in zip(ins, steps):
                    outs[0][start:start + height(step), :] = ref[...]
                    start += height(step)

            total = sum(height(step) for step in steps)
            return chain.run("packed", body, [shape(total, units)], [hidden[step] for step in steps], False)[0]

        def packed_stream():
            def body(ins, outs):
                for side in range(2):
                    start = 0
                    for ref, step in zip(ins[side::2], order):
                        size = height(step)
                        source = half_at(0, half) if step == 0 else pl.ds(0, size)
                        outs[side][start:start + size, :] = ref[source, 0:width]
                        outs[2][side * share + start:side * share + start + size, :] = ref[source, width:2 * width]
                        start += size

            outs = [shape(share, width)] * 2 + [shape(2 * share, width)]
            tok, cot, give = chain.run("packed", body, outs, [block for step in order for block in blocks[step]], False)
            return tok, cot, to_sibling(give)

        sums, act, slope, dpre, act_term, act_far, dpre_far = {}, {}, {}, {}, {}, {}, {}
        blocks = {step: [None, None] for step in range(far + 1)}
        everything = slice(None)

        stream = [to_sibling(tokens), to_sibling(cotangent)]
        came = own_other()
        blocks[0] = both_bands(stream)
        blocks[1] = [outward(block) for block in blocks[0]]
        own_mine(came)
        w_in_far, w_out_far = (to_sibling(weight) for weight in held([w_in, w_out]))

        for step in range(1, far + 1):
            if step < far:
                relay(step, 0)
            product(step, 0)
            if step < far:
                gelu(step - 1, [act_far[step - 2]] if step > 1 else [])
                relay(step, 1)
            if step == 1:
                w_in_t, w_in_t_far = turned(w_in), turned(w_in_far)
            if step == 2:
                w_out_t, w_out_t_far = turned(w_out), turned(w_out_far)
            elif 2 < step < far:
                act_term[step - 3] = term(step - 3, act, (w_out, w_out_far))
        product(far, 1)
        act_term[max(far - 3, 0)] = term(max(far - 3, 0), act, (w_out, w_out_far))
        arrived([*sums[0, far - 1], act_far[far - 2]])
        tok_own, cot_own, stream_far = packed_stream()
        gelu(far - 1)
        for step in range(max(far - 3, 0) + 1, far):
            act_term[step] = term(step, act, (w_out, w_out_far))
        product(far - 1, 1)
        gelu(far, [act_far[far - 1], stream_far])
        going = homeward(term(far, act, (w_out, w_out_far)))
        back_going = grad_out = None
        for step in range(far, 1, -1):
            slopes(step, [act_far[far] if step == far else dpre_far[step + 1]])
            back_going = homeward(term(step, dpre, (w_in_t, w_in_t_far), back_going))
            going = homeward(joined(step - 1, act_term[step - 1], going))
            product(step - 2, 1)
            if far - 1 <= step:
                grad_out = chain.outer("grad_out", [
                    (packed_hidden(act, order), everything, cot_own, everything),
                    (packed_hidden(act_far, order), everything, stream_far, pl.ds(share, share)),
                ], grad_out, (far - step, 2))
        slopes(1, [dpre_far[2]])
        back_going = homeward(term(1, dpre, (w_in_t, w_in_t_far), back_going))
        row_shares = halved(act_term[0], going)
        slopes(0)
        back_own = term(0, dpre, (w_in_t, w_in_t_far))
        bands = spread(*row_shares)
        dpre_own, dpre_other = packed_hidden(dpre, order), packed_hidden(dpre_far, order)
        grad_in = None
        for index in range(2):
            grad_in = chain.outer("grad_in", [
                (tok_own, everything, dpre_own, everything),
                (stream_far, pl.ds(0, share), dpre_other, everything),
            ], grad_in, (index, 2))
            if index == 0:
                keep, came = settled(back_own, back_going)
        block_out, grad_tokens = finish(bands, [cotangent, keep, came])
        return block_out, grad_tokens, grad_in, grad_out

    in_specs = (P("row", "col"), P("col", "row"), P("row", "col"), P("row", "col"))
    out_specs = (P(("row", "col"), None), P("row", "col"), P("col", "row"), P("row", "col"))
    return jax.shard_map(local, mesh=mesh, in_specs=in_specs, out_specs=out_specs, check_vma=False)
```
